512 devices in a mesh: tower: 16 (over z, core), seq: 8 (over y), mp: 4 (over x).
Axes of the slice: x: 4, y: 8, z: 8, core: 2. Of those that a mesh axis runs over, the one named last changes fastest.
Arguments:
- tiles: bfloat16 [256, 8, 8, 3072], P(('tower', 'mp'), None, None, 'seq'), may hold values from -6 to 6
- dw_weight: float32 [7, 7, 3072], P(None, None, 'seq'), may hold values from -0.875 to 0.875
- dw_bias: float32 [3072], P('seq'), may hold values from -3 to 3
- block_gain: float32 [3072], P('seq'), may hold values from 0.5 to 1.5
- block_bias: float32 [3072], P('seq'), may hold values from -3 to 3
- proj_weight: bfloat16 [3072, 8192], P('seq', 'mp'), may hold values from -0.109375 to 0.109375
- proj_bias: float32 [8192], P('mp'), may hold values from -3 to 3
- directions: float32 [16, 8192], replicated, may hold values from 0.001 to 30
- dir_index: int32 [16], P('tower'), may hold values from 0 to 15
- tile_counts: int32 [16], P('tower'), may hold values from 1 to 16
- positions: int32 [16, 1024], P('tower', 'seq'), may hold values from 0 to 5118, as said below
- rms_gain: float32 [8192], P('mp'), may hold values from 0.5 to 1.5
- kv_weight: bfloat16 [2, 8192, 1024], P(None, 'tower', 'mp'), may hold values from -0.0625 to 0.0625
- kv_bias: float32 [2, 1024], P(None, 'mp'), may hold values from -3 to 3
Outputs:
- cache: bfloat16 [16, 2, 1024, 1024], P('tower', None, 'seq', 'mp')
The draws below stay inside these ranges and needn't reach their ends.
Inputs may be any that keep to these rules, and one draw needn't show every extreme that they name: Each request's visual token slots take 1024 consecutive increasing positions.
All inputs are finite; a program needn't handle non-finite values.
Results may differ from the reference program's by a relative error of at most 0.02.
Values may be sent and summed in bfloat16 or wider, within the bound.
No kernel may reach another device: no remote copies, remote signals or barrier semaphores. Data moves between devices by JAX's collectives and lax.ppermute only.
A program may use at most 64 MiB of HBM per device.

```python
import jax
import jax.numpy as jnp
from jax import lax

C = 3072
D = 8192
HEAD = 128
KER = 7
SIDE = 8
MAXT = 16
NDIR = 16
REQ = 16
VIS = 1024
KVW = 1024
N_SEQ = 8


def draw_positions(key, part):
    key = jax.random.fold_in(key, 11)
    begins = jax.random.randint(key, (REQ, 1), 0, 4096, dtype=jnp.int32)
    high_req = jax.random.randint(jax.random.fold_in(key, 12), (), 0, REQ, dtype=jnp.int32)
    low_step = jax.random.randint(jax.random.fold_in(key, 13), (), 1, REQ, dtype=jnp.int32)
    low_req = (high_req + low_step) % REQ
    request_ids = jnp.arange(REQ, dtype=jnp.int32)[:, None]
    begins = jnp.where(request_ids == high_req, jnp.int32(4095), begins)
    begins = jnp.where(request_ids == low_req, jnp.int32(0), begins)
    return (begins + jnp.arange(VIS, dtype=jnp.int32)[None, :]).astype(jnp.int32)


def draw_directions(key, part):
    key = jax.random.fold_in(key, 21)
    uniform_part = jax.random.uniform(key, (NDIR, D), jnp.float32)
    entries = jnp.exp(jnp.log(jnp.float32(0.01)) + uniform_part * jnp.log(jnp.float32(100.0)))
    top_scale = 10.0
    column_pos = jnp.arange(D, dtype=jnp.float32) / jnp.float32(D - 1)
    column_scale = jnp.exp(column_pos * jnp.log(jnp.float32(top_scale)))
    return (entries * column_scale[None, :]).astype(jnp.float32)


def place_ends(values, rng, smallest, high):
    extent = values.shape
    place = [jax.random.randint(jax.random.fold_in(rng, axis), (), 0, extent[axis]) for axis in range(len(extent))]
    values = values.at[tuple(place)].set(smallest)
    longest = extent.index(max(extent))
    place[longest] = (place[longest] + 1) % extent[longest]
    return values.at[tuple(place)].set(high)


def shard_levels(own_key, extent, cuts, least, high):
    level = 1.0
    for dim, shards_of in cuts:
        steps = jax.random.uniform(jax.random.fold_in(jax.random.fold_in(own_key, 6), dim), (shards_of,), jnp.float32, least / len(cuts), high / len(cuts))
        level = level * jnp.repeat(jnp.exp(steps), extent[dim] // shards_of).reshape((-1,) + (1,) * (len(extent) - 1 - dim))
    return level


def bell_draw(stream_key, shape, deviation, most, split=(), kind=jnp.bfloat16):
    values = deviation * jax.random.normal(stream_key, shape, jnp.float32)
    if split:
        values = values * shard_levels(stream_key, shape, split, -0.22, 0.18)
    return jnp.clip(values, -most, most).astype(kind)


def setup_inputs(seed: int = 0) -> dict:
    keys = jax.random.split(jax.random.key(seed), 15)
    return {
        "tiles": bell_draw(keys[0], (REQ * MAXT, SIDE, SIDE, C), 1.0, 6.0, ((0, 64), (3, 8))),
        "dw_weight": bell_draw(keys[1], (KER, KER, C), (KER * KER) ** -0.5, 0.875, ((2, 8),), jnp.float32),
        "dw_bias": bell_draw(keys[2], (C,), 0.5, 3.0, ((0, 8),), jnp.float32),
        "block_gain": jnp.clip(1.0 + 0.1 * jax.random.normal(keys[3], (C,), jnp.float32), 0.5, 1.5),
        "block_bias": bell_draw(keys[4], (C,), 0.5, 3.0, ((0, 8),), jnp.float32),
        "proj_weight": bell_draw(keys[5], (C, D), C ** -0.5, 0.109375, ((0, 8), (1, 4))),
        "proj_bias": bell_draw(keys[6], (D,), 0.5, 3.0, ((0, 4),), jnp.float32),
        "directions": draw_directions(jax.random.fold_in(keys[14], 71), 0),
        "dir_index": place_ends(jax.random.randint(keys[8], (REQ,), 0, NDIR), jax.random.fold_in(keys[8], 1), 0, NDIR - 1).astype(jnp.int32),
        "tile_counts": place_ends(jax.random.randint(keys[9], (REQ,), 1, MAXT + 1), jax.random.fold_in(keys[9], 1), 1, MAXT).astype(jnp.int32),
        "positions": draw_positions(jax.random.fold_in(keys[14], 71), 0),
        "rms_gain": jnp.clip(1.0 + 0.1 * jax.random.normal(keys[11], (D,), jnp.float32), 0.5, 1.5),
        "kv_weight": bell_draw(keys[12], (2, D, KVW), D ** -0.5, 0.0625, ((1, 16), (2, 4))),
        "kv_bias": bell_draw(keys[13], (2, KVW), 0.5, 3.0, ((1, 4),), jnp.float32),
    }


epsilon = 1e-06

def depthwise(inputs, kernel, shift):
    reach = kernel.shape[0] // 2
    cells = inputs.shape[1]
    padded = jnp.pad(inputs, ((0, 0), (reach, reach), (reach, reach), (0, 0)))
    running = jnp.zeros_like(inputs) + shift
    for row_off in range(kernel.shape[0]):
        for col_off in range(kernel.shape[1]):
            running = running + padded[:, row_off:row_off + cells, col_off:col_off + cells, :] * kernel[row_off, col_off]
    return running

def rotate(key_rows, position):
    count_rows = key_rows.shape[0]
    heads = key_rows.reshape(count_rows, -1, HEAD)
    half_head = HEAD // 2
    inverse = jnp.power(jnp.float32(1000000.0), -(jnp.arange(half_head, dtype=jnp.float32) * 2.0 / HEAD))
    angles = position.astype(jnp.float32)[:, None] * inverse[None, :]
    cosine = jnp.cos(angles)[:, None, :]
    sine_part = jnp.sin(angles)[:, None, :]
    leading = heads[..., :half_head]
    trailing = heads[..., half_head:]
    turned = jnp.concatenate([leading * cosine - trailing * sine_part, trailing * cosine + leading * sine_part], axis=-1)
    return turned.reshape(count_rows, -1)

def reference(tiles, dw_weight, dw_bias, block_gain, block_bias, proj_weight, proj_bias, directions, dir_index, tile_counts, positions, rms_gain, kv_weight, kv_bias):
    grouped = tiles.reshape(REQ, MAXT, SIDE, SIDE, C)

    def one_request(packed):
        request_tiles, count_tiles, chosen_index, position = packed
        inputs = request_tiles.astype(jnp.float32)
        filtered = depthwise(inputs, dw_weight, dw_bias)
        average = lax.optimization_barrier(jnp.mean(filtered, -1, keepdims=True))
        variance = lax.optimization_barrier(jnp.mean(filtered * filtered, -1, keepdims=True)) - average * average
        normalized = (filtered - average) * lax.rsqrt(variance + epsilon) * block_gain + block_bias
        block_rows = normalized.astype(jnp.bfloat16).reshape(VIS, C)
        block_width = C // N_SEQ
        projected = jnp.zeros((VIS, D), jnp.float32)
        for block in range(N_SEQ):
            partial_sum = jnp.dot(block_rows[:, block * block_width:(block + 1) * block_width], proj_weight[block * block_width:(block + 1) * block_width], preferred_element_type=jnp.float32)
            rounded = lax.optimization_barrier(partial_sum.astype(jnp.bfloat16))
            projected = projected + rounded.astype(jnp.float32)
        hidden = jax.nn.gelu(projected + proj_bias, approximate=False)
        chosen = directions[chosen_index]
        unit_dir = chosen / jnp.sqrt(jnp.sum(chosen * chosen))
        coefficient = lax.optimization_barrier(jnp.sum(hidden * unit_dir, -1, keepdims=True))
        ablated = hidden - coefficient * unit_dir
        mean_square = lax.optimization_barrier(jnp.mean(ablated * ablated, -1, keepdims=True))
        normed = (ablated * lax.rsqrt(mean_square + epsilon) * rms_gain).astype(jnp.bfloat16)
        key_rows = jnp.dot(normed, kv_weight[0], preferred_element_type=jnp.float32) + kv_bias[0]
        values = jnp.dot(normed, kv_weight[1], preferred_element_type=jnp.float32) + kv_bias[1]
        key_rows = rotate(key_rows, position)
        row_valid = (jnp.arange(VIS, dtype=jnp.int32) // (SIDE * SIDE) < count_tiles).astype(jnp.float32)[:, None]
        return (jnp.stack([key_rows, values]) * row_valid).astype(jnp.bfloat16)
    return lax.map(one_request, (grouped, tile_counts, dir_index, positions))
```

```python
import jax
import jax.numpy as jnp
from jax import lax
from jax.experimental import pallas as pl
from jax.experimental.pallas import tpu as pltpu
from jax.sharding import PartitionSpec as P

C = 3072
D = 8192
HEAD = 128
SIDE = 8


epsilon = 1e-06


def depthwise(inputs, kernel, shift):
    reach = kernel.shape[0] // 2
    cells = inputs.shape[1]
    padded = jnp.pad(inputs, ((0, 0), (reach, reach), (reach, reach), (0, 0)))
    running = jnp.zeros_like(inputs) + shift
    for row_off in range(kernel.shape[0]):
        for col_off in range(kernel.shape[1]):
            running = (
                running
                + padded[:, row_off : row_off + cells, col_off : col_off + cells, :]
                * kernel[row_off, col_off]
            )
    return running


def rotate(key_rows, position):
    count_rows = key_rows.shape[0]
    heads = key_rows.reshape(count_rows, -1, HEAD)
    half_head = HEAD // 2
    inverse = jnp.power(
        jnp.float32(1000000.0), -(jnp.arange(half_head, dtype=jnp.float32) * 2.0 / HEAD)
    )
    angles = position.astype(jnp.float32)[:, None] * inverse[None, :]
    cosine = jnp.cos(angles)[:, None, :]
    sine_part = jnp.sin(angles)[:, None, :]
    leading = heads[..., :half_head]
    trailing = heads[..., half_head:]
    turned = jnp.concatenate(
        [leading * cosine - trailing * sine_part, trailing * cosine + leading * sine_part], axis=-1
    )
    return turned.reshape(count_rows, -1)


def split_dot(rows, weight):
    parts = []
    rest = rows
    for _ in range(3):
        part = lax.reduce_precision(rest, 8, 7)
        parts.append(part)
        rest = rest - part
    stacked = jnp.concatenate(parts, 0).astype(jnp.bfloat16)
    out = jnp.dot(stacked, weight, preferred_element_type=jnp.float32)
    count = rows.shape[0]
    return out[:count] + out[count : 2 * count] + out[2 * count :]


def kv_kernel(rows_ref, weight_ref, out_ref):
    blocks, _, depth, width = weight_ref.shape
    for pair in range(2):
        total = jnp.zeros((rows_ref.shape[0], width), jnp.float32)
        for block in range(blocks):
            total = total + jnp.dot(
                rows_ref[:, block * depth : (block + 1) * depth],
                weight_ref[block, pair],
                preferred_element_type=jnp.float32,
            )
        out_ref[0, :, pair * width : (pair + 1) * width] = total.astype(out_ref.dtype)


def kv_partial(rows, weight):
    count = rows.shape[0]
    _, pairs, depth, width = weight.shape
    blocks = rows.shape[1] // depth
    groups = weight.shape[0] // blocks
    return pl.pallas_call(
        kv_kernel,
        grid=(groups,),
        in_specs=[
            pl.BlockSpec((count, rows.shape[1]), lambda g: (0, 0)),
            pl.BlockSpec((blocks, pairs, depth, width), lambda g: (g, 0, 0, 0)),
        ],
        out_specs=pl.BlockSpec((1, count, pairs * width), lambda g: (g, 0, 0)),
        out_shape=jax.ShapeDtypeStruct((groups, count, pairs * width), jnp.bfloat16),
        compiler_params=pltpu.CompilerParams(vmem_limit_bytes=56 * 2**20),
    )(rows, weight)


def local(
    tiles,
    dw_weight,
    dw_bias,
    block_gain,
    block_bias,
    proj_weight,
    proj_bias,
    directions,
    dir_index,
    tile_counts,
    positions,
    rms_gain,
    kv_weight,
    kv_bias,
):
    n_seq = lax.axis_size("seq")
    n_mp = lax.axis_size("mp")
    n_tower = lax.axis_size("tower")
    inner = n_tower // n_mp
    swap = [
        ((a * inner + b) * n_mp + x, (x * inner + b) * n_mp + a)
        for a in range(n_mp)
        for b in range(inner)
        for x in range(n_mp)
    ]
    swapped = lax.ppermute(kv_weight, ("tower", "mp"), swap)

    inputs = tiles.astype(jnp.float32)
    filtered = depthwise(inputs, dw_weight, dw_bias)
    channels = inputs.shape[3]
    mean_here = jnp.sum(filtered, -1) / channels
    centered = filtered - mean_here[..., None]
    square_here = jnp.sum(centered * centered, -1)
    block_rows = (centered * block_gain).astype(jnp.bfloat16).reshape(-1, channels)
    gathered = lax.all_gather(block_rows, "mp", axis=0, tiled=True)
    gathered, swapped = lax.optimization_barrier((gathered, swapped))
    kv_rows = lax.all_gather(swapped, "tower", axis=0, tiled=False)
    partial = jnp.dot(gathered, proj_weight, preferred_element_type=jnp.float32).astype(
        jnp.bfloat16
    )
    vectors = split_dot(jnp.stack([block_gain, block_bias]), proj_weight)
    partial, mean_here, square_here, vectors = lax.optimization_barrier(
        (partial, mean_here, square_here, vectors)
    )
    summed = lax.psum_scatter(partial, "seq", scatter_dimension=0, tiled=True)

    stats = jnp.stack([mean_here.reshape(-1), square_here.reshape(-1)])
    stats = lax.all_gather(stats, "mp", axis=1, tiled=True)
    rows_here = stats.shape[1] // n_seq
    stats = stats.reshape(2, n_seq, rows_here).swapaxes(0, 1).reshape(n_seq, -1)
    payload = jnp.concatenate(
        [stats, jnp.broadcast_to(vectors.reshape(1, -1), (n_seq, vectors.size))], 1
    )
    payload = lax.all_to_all(payload, "seq", 0, 0, tiled=True)
    means = payload[:, :rows_here]
    squares = payload[:, rows_here : 2 * rows_here]
    column_count = vectors.shape[1]
    gain_rows = payload[:, 2 * rows_here : 2 * rows_here + column_count]
    bias_row = jnp.sum(payload[:, 2 * rows_here + column_count :], 0) + proj_bias
    average = jnp.sum(means, 0) / n_seq
    offsets = means - average
    variance = (jnp.sum(squares, 0) + channels * jnp.sum(offsets * offsets, 0)) / C
    inverse_std = lax.rsqrt(variance + epsilon)
    shift = jnp.dot(offsets.T, gain_rows, precision=lax.Precision.HIGHEST)

    picked = jnp.arange(directions.shape[0], dtype=jnp.int32)[:, None] == dir_index[0]
    chosen = jnp.sum(jnp.where(picked, directions, 0.0), 0)
    unit_dir = chosen / jnp.sqrt(jnp.sum(chosen * chosen))
    local_unit = lax.dynamic_slice_in_dim(
        unit_dir, lax.axis_index("mp") * column_count, column_count, 0
    )
    unit_square = jnp.sum(local_unit * local_unit)

    projected = (summed.astype(jnp.float32) + shift) * inverse_std[:, None]
    hidden = jax.nn.gelu(projected + bias_row, approximate=False)
    along_unit = jnp.sum(hidden * local_unit, -1)
    part = along_unit / unit_square
    across = hidden - part[:, None] * local_unit
    across_square = jnp.sum(across * across, -1)
    norms = lax.all_gather(
        jnp.concatenate([along_unit, across_square, jnp.broadcast_to(unit_square, (128,))]),
        "mp",
        axis=0,
        tiled=False,
    )
    along_all = norms[:, :rows_here]
    across_all = norms[:, rows_here : 2 * rows_here]
    unit_all = norms[:, 2 * rows_here : 2 * rows_here + 1]
    coefficient = jnp.sum(along_all, 0)
    left = along_all / unit_all - coefficient
    mean_square = (jnp.sum(across_all, 0) + jnp.sum(left * left * unit_all, 0)) / D
    ablated = across + (part - coefficient)[:, None] * local_unit
    normed = (ablated * lax.rsqrt(mean_square + epsilon)[:, None] * rms_gain).astype(jnp.bfloat16)

    pieces = kv_partial(normed, kv_rows)
    pieces = lax.all_to_all(pieces, "mp", 0, 0, tiled=True)
    kv_pair = jnp.sum(pieces.astype(jnp.float32), 0)
    width = kv_bias.shape[1]
    key_rows = rotate(kv_pair[:, :width] + kv_bias[0], positions[0])
    values = kv_pair[:, width:] + kv_bias[1]
    row_ids = lax.axis_index("seq") * rows_here + jnp.arange(rows_here, dtype=jnp.int32)
    row_valid = (row_ids // (SIDE * SIDE) < tile_counts[0]).astype(jnp.float32)[:, None]
    return (jnp.stack([key_rows, values]) * row_valid)[None].astype(jnp.bfloat16)


def solution(mesh):
    return jax.shard_map(
        local,
        mesh=mesh,
        in_specs=(
            P(("tower", "mp"), None, None, "seq"),
            P(None, None, "seq"),
            P("seq"),
            P("seq"),
            P("seq"),
            P("seq", "mp"),
            P("mp"),
            P(),
            P("tower"),
            P("tower"),
            P("tower", "seq"),
            P("mp"),
            P(None, "tower", "mp"),
            P(None, "mp"),
        ),
        out_specs=P("tower", None, "seq", "mp"),
        check_vma=False,
    )
```

```python
import jax
import jax.numpy as jnp
from jax import lax
from jax.experimental import pallas as pl
from jax.experimental.pallas import tpu as pltpu
from jax.sharding import PartitionSpec as P

C = 3072
D = 8192
HEAD = 128
SIDE = 8


epsilon = 1e-06


def conv_kernel(tile_ref, weight_ref, shift_ref, gain_ref, rows_ref, stats_ref, held):
    _, cells, width, channels = tile_ref.shape
    side = weight_ref.shape[0]
    reach = side // 2
    lanes = 128
    total = jnp.zeros((cells, width, 1), jnp.float32)
    column = lax.broadcasted_iota(jnp.int32, (cells, width, lanes), 1)
    for group in range(channels // lanes):
        part = slice(group * lanes, (group + 1) * lanes)
        cell = tile_ref[0, :, :, part].astype(jnp.float32)
        sums = [
            jnp.broadcast_to(shift_ref[:, part], (width, lanes)) for _ in range(cells)
        ]
        for col_off in range(side):
            move = col_off - reach
            moved = cell
            if move:
                inside = (column + move >= 0) & (column + move < width)
                moved = jnp.where(inside, pltpu.roll(cell, (-move) % width, 1), 0.0)
            for row_off in range(side):
                scale = jnp.broadcast_to(
                    weight_ref[row_off, col_off : col_off + 1, part], (width, lanes)
                )
                for row in range(cells):
                    source = row + row_off - reach
                    if 0 <= source < cells:
                        sums[row] = sums[row] + moved[source] * scale
        out = jnp.stack(sums)
        held[:, :, part] = out
        total = total + jnp.sum(out, -1, keepdims=True)
    average = total / channels
    square = jnp.zeros((cells, width, 1), jnp.float32)
    for group in range(channels // lanes):
        part = slice(group * lanes, (group + 1) * lanes)
        centered = held[:, :, part] - average
        square = square + jnp.sum(centered * centered, -1, keepdims=True)
        rows_ref[0, :, :, part] = (centered * gain_ref[0, part]).astype(rows_ref.dtype)
    stats_ref[0, 0] = jnp.broadcast_to(average, (cells, width, lanes))
    stats_ref[1, 0] = jnp.broadcast_to(square, (cells, width, lanes))


def conv_rows(tiles, kernel, shift, gain):
    count, cells, width, channels = tiles.shape
    whole = pl.BlockSpec((1, channels), lambda t: (0, 0))
    return pl.pallas_call(
        conv_kernel,
        grid=(count,),
        in_specs=[
            pl.BlockSpec((1, cells, width, channels), lambda t: (t, 0, 0, 0)),
            pl.BlockSpec(kernel.shape, lambda t: (0, 0, 0)),
            whole,
            whole,
        ],
        out_specs=[
            pl.BlockSpec((1, cells, width, channels), lambda t: (t, 0, 0, 0)),
            pl.BlockSpec((2, 1, cells, width, 128), lambda t: (0, t, 0, 0, 0)),
        ],
        out_shape=[
            jax.ShapeDtypeStruct(tiles.shape, jnp.bfloat16),
            jax.ShapeDtypeStruct((2, count, cells, width, 128), jnp.float32),
        ],
        scratch_shapes=[pltpu.VMEM((cells, width, channels), jnp.float32)],
        compiler_params=pltpu.CompilerParams(vmem_limit_bytes=32 * 2**20),
    )(tiles, kernel, shift[None], gain[None])


def split_dot(rows, weight):
    parts = []
    rest = rows
    for _ in range(3):
        part = lax.reduce_precision(rest, 8, 7)
        parts.append(part)
        rest = rest - part
    stacked = jnp.concatenate(parts, 0).astype(jnp.bfloat16)
    out = jnp.dot(stacked, weight, preferred_element_type=jnp.float32)
    count = rows.shape[0]
    return out[:count] + out[count : 2 * count] + out[2 * count :]


def three_parts(value):
    first = value.astype(jnp.bfloat16).astype(jnp.float32)
    rest = value - first
    second = rest.astype(jnp.bfloat16).astype(jnp.float32)
    return first, second, rest - second


EXTRA = 16
STEP = 16


def kv_kernel(
    summed_ref, means_ref, squares_ref, gains_ref, bias_ref, unit_ref, scale_ref, weight_ref,
    out_ref, rows, stats,
):
    count, features = summed_ref.shape
    towers, _, _, depth, width = weight_ref.shape
    n_seq = means_ref.shape[0]
    inner = features // depth // 4

    @pl.when(pl.program_id(0) == 0)
    def _():
        means = means_ref[...]
        average = jnp.sum(means, 0, keepdims=True) / n_seq
        offsets = means - average
        block = C // n_seq
        variance = (
            jnp.sum(squares_ref[...], 0, keepdims=True)
            + block * jnp.sum(offsets * offsets, 0, keepdims=True)
        ) / C
        inverse = lax.rsqrt(variance + epsilon)
        columns = jnp.transpose(
            jnp.concatenate([offsets, jnp.broadcast_to(inverse, (n_seq, count))], 0)
        )
        unit = unit_ref[...]
        gain = scale_ref[...]
        unit_square = jnp.sum(unit * unit)
        for begin in range(0, count, STEP):
            here = slice(begin, begin + STEP)
            value = summed_ref[here, :].astype(jnp.float32)
            for source in range(n_seq):
                value = value + columns[here, source : source + 1] * gains_ref[source : source + 1, :]
            value = value * columns[here, n_seq : n_seq + 1] + bias_ref[...]
            hidden = 0.5 * value * (1.0 + lax.erf(value * 0.7071067811865476))
            along = jnp.sum(hidden * unit, -1, keepdims=True)
            across = hidden - (along / unit_square) * unit
            square = jnp.sum(across * across, -1, keepdims=True)
            lane = lax.broadcasted_iota(jnp.int32, (STEP, count), 1)
            stats[here, :] = jnp.where(lane == 0, along, jnp.where(lane == 1, square, unit_square))
            scaled = (across * gain).astype(jnp.bfloat16)
            for place in range(features // depth):
                first, second = place // inner, place % inner
                source = second * 4 + first
                rows[here, place * depth : (place + 1) * depth] = scaled[
                    :, source * depth : (source + 1) * depth
                ]
        parts = jnp.concatenate(
            [*three_parts(unit * gain), jnp.zeros((EXTRA - 3, features), jnp.float32)], 0
        ).astype(jnp.bfloat16)
        for place in range(features // depth):
            first, second = place // inner, place % inner
            source = second * 4 + first
            rows[count:, place * depth : (place + 1) * depth] = parts[
                :, source * depth : (source + 1) * depth
            ]

    turned = jnp.transpose(stats[...])[:8]
    for pair in range(2):
        there = slice(pair * width, (pair + 1) * width)
        weight = weight_ref[:, 0, pair].reshape(towers * depth, width)
        total = jnp.dot(rows[...], weight, preferred_element_type=jnp.float32)
        out_ref[0, :count, there] = total[:count].astype(out_ref.dtype)
        vector = total[count : count + 1] + total[count + 1 : count + 2] + total[count + 2 : count + 3]
        line = jnp.concatenate([turned[pair : pair + 1], turned[2:3]], 1)
        extra = jnp.concatenate(
            [
                *three_parts(vector),
                *three_parts(line),
                jnp.zeros((EXTRA - 6, width), jnp.float32),
            ],
            0,
        )
        out_ref[0, count:, there] = extra.astype(out_ref.dtype)


def kv_partial(summed, means, squares, gains, bias, unit, scale, weight):
    count, features = summed.shape
    towers, groups, pairs, depth, width = weight.shape

    def whole(array):
        return pl.BlockSpec(array.shape, lambda g: (0,) * array.ndim)

    return pl.pallas_call(
        kv_kernel,
        grid=(groups,),
        in_specs=[
            *(whole(a) for a in (summed, means, squares, gains, bias, unit, scale)),
            pl.BlockSpec((towers, 1, pairs, depth, width), lambda g: (0, g, 0, 0, 0)),
        ],
        out_specs=pl.BlockSpec((1, count + EXTRA, pairs * width), lambda g: (g, 0, 0)),
        out_shape=jax.ShapeDtypeStruct((groups, count + EXTRA, pairs * width), jnp.bfloat16),
        scratch_shapes=[
            pltpu.VMEM((count + EXTRA, features), jnp.bfloat16),
            pltpu.VMEM((count, count), jnp.float32),
        ],
        compiler_params=pltpu.CompilerParams(vmem_limit_bytes=56 * 2**20),
    )(summed, means, squares, gains, bias, unit, scale, weight)


def end_kernel(pieces_ref, bias_ref, cosine_ref, sine_ref, valid_ref, out_ref):
    groups, rows, both = pieces_ref.shape
    count = rows - EXTRA
    width = both // 2
    extra = pieces_ref[:, count:, :].astype(jnp.float32)
    vectors = extra[:, 0] + extra[:, 1] + extra[:, 2]
    lines = extra[:, 3] + extra[:, 4] + extra[:, 5]
    along = lines[:, :count]
    unit_square = lines[:, count : 2 * count]
    across = lines[:, width : width + count]
    coefficient = jnp.sum(along, 0, keepdims=True)
    left = along / unit_square - coefficient
    mean_square = jnp.sum(across + left * left * unit_square, 0, keepdims=True) / D
    inverse = lax.rsqrt(mean_square + epsilon)
    columns = jnp.transpose(
        jnp.concatenate([left, jnp.broadcast_to(inverse, (8 - groups, count))], 0)
    )
    total = jnp.zeros((count, both), jnp.float32)
    for group in range(groups):
        total = total + pieces_ref[group, :count].astype(jnp.float32)
        total = total + columns[:, group : group + 1] * vectors[group : group + 1, :]
    total = total * columns[:, groups : groups + 1]
    valid = valid_ref[...]
    for head in range(width // HEAD):
        there = slice(head * HEAD, (head + 1) * HEAD)
        key = total[:, there] + bias_ref[0:1, there]
        turned = key * cosine_ref[...] + pltpu.roll(key, HEAD // 2, 1) * sine_ref[...]
        out_ref[0, 0, :, there] = (turned * valid).astype(out_ref.dtype)
    value = total[:, width:] + bias_ref[1:2, :]
    out_ref[0, 1] = (value * valid[:, :1]).astype(out_ref.dtype)


def end_rows(pieces, bias, cosine, sine, valid):
    _, rows, both = pieces.shape
    return pl.pallas_call(
        end_kernel,
        out_shape=jax.ShapeDtypeStruct((1, 2, rows - EXTRA, both // 2), jnp.bfloat16),
        compiler_params=pltpu.CompilerParams(vmem_limit_bytes=32 * 2**20),
    )(pieces, bias, cosine, sine, valid)


def local(
    tiles,
    dw_weight,
    dw_bias,
    block_gain,
    block_bias,
    proj_weight,
    proj_bias,
    directions,
    dir_index,
    tile_counts,
    positions,
    rms_gain,
    kv_weight,
    kv_bias,
):
    n_seq = lax.axis_size("seq")
    n_mp = lax.axis_size("mp")
    n_tower = lax.axis_size("tower")
    pairs, depth, width = kv_weight.shape
    inner = n_tower // n_mp
    cut = kv_weight.reshape(pairs, n_mp, depth // n_mp, width).swapaxes(0, 1)
    cut = lax.all_to_all(
        cut,
        "tower",
        0,
        0,
        tiled=True,
        axis_index_groups=[[a * inner + b for a in range(n_mp)] for b in range(inner)],
    )

    block_rows, stats = conv_rows(tiles, dw_weight, dw_bias, block_gain)
    channels = tiles.shape[3]
    gathered = lax.all_gather(block_rows.reshape(-1, channels), "mp", axis=0, tiled=True)
    gathered, cut = lax.optimization_barrier((gathered, cut))
    kv_rows = lax.all_gather(
        lax.all_to_all(cut, "mp", 0, 0, tiled=True), "tower", axis=0, tiled=False
    )
    partial = jnp.dot(gathered, proj_weight, preferred_element_type=jnp.float32).astype(
        jnp.bfloat16
    )
    partial, stats, block_gain, block_bias = lax.optimization_barrier(
        (partial, stats, block_gain, block_bias)
    )
    summed = lax.psum_scatter(partial, "seq", scatter_dimension=0, tiled=True)

    vectors = split_dot(jnp.stack([block_gain, block_bias]), proj_weight)
    stats = stats[..., 0].reshape(2, -1)
    stats = lax.all_gather(stats, "mp", axis=1, tiled=True)
    rows_here = stats.shape[1] // n_seq
    stats = stats.reshape(2, n_seq, rows_here).swapaxes(0, 1).reshape(n_seq, -1)
    payload = jnp.concatenate(
        [stats, jnp.broadcast_to(vectors.reshape(1, -1), (n_seq, vectors.size))], 1
    )
    payload = lax.all_to_all(payload, "seq", 0, 0, tiled=True)
    means = payload[:, :rows_here]
    squares = payload[:, rows_here : 2 * rows_here]
    column_count = vectors.shape[1]
    gain_rows = payload[:, 2 * rows_here : 2 * rows_here + column_count]
    bias_row = jnp.sum(payload[:, 2 * rows_here + column_count :], 0) + proj_bias

    picked = jnp.arange(directions.shape[0], dtype=jnp.int32)[:, None] == dir_index[0]
    chosen = jnp.sum(jnp.where(picked, directions, 0.0), 0)
    unit_dir = chosen / jnp.sqrt(jnp.sum(chosen * chosen))
    local_unit = lax.dynamic_slice_in_dim(
        unit_dir, lax.axis_index("mp") * column_count, column_count, 0
    )

    half_head = HEAD // 2
    inverse = jnp.power(
        jnp.float32(1000000.0), -(jnp.arange(half_head, dtype=jnp.float32) * 2.0 / HEAD)
    )
    angles = positions[0].astype(jnp.float32)[:, None] * inverse[None, :]
    cosine = jnp.tile(jnp.cos(angles), (1, 2))
    sine_part = jnp.sin(angles)
    sine = jnp.concatenate([-sine_part, sine_part], 1)
    row_ids = lax.axis_index("seq") * rows_here + jnp.arange(rows_here, dtype=jnp.int32)
    row_valid = (row_ids // (SIDE * SIDE) < tile_counts[0]).astype(jnp.float32)[:, None]
    row_valid = jnp.broadcast_to(row_valid, cosine.shape)

    pieces = kv_partial(
        summed,
        means,
        squares,
        gain_rows,
        bias_row[None],
        local_unit[None],
        rms_gain[None],
        kv_rows,
    )
    pieces = lax.all_to_all(pieces, "mp", 0, 0, tiled=True)
    return end_rows(pieces, kv_bias, cosine, sine, row_valid)


def solution(mesh):
    return jax.shard_map(
        local,
        mesh=mesh,
        in_specs=(
            P(("tower", "mp"), None, None, "seq"),
            P(None, None, "seq"),
            P("seq"),
            P("seq"),
            P("seq"),
            P("seq", "mp"),
            P("mp"),
            P(),
            P("tower"),
            P("tower"),
            P("tower", "seq"),
            P("mp"),
            P(None, "tower", "mp"),
            P(None, "mp"),
        ),
        out_specs=P("tower", None, "seq", "mp"),
        check_vma=False,
    )
```

```python
import jax
import jax.numpy as jnp
from jax import lax
from jax.experimental import pallas as pl
from jax.experimental.pallas import tpu as pltpu
from jax.sharding import PartitionSpec as P

C = 3072
D = 8192
HEAD = 128
SIDE = 8
INNER = 4


epsilon = 1e-06


def conv_kernel(tile_ref, weight_ref, shift_ref, gain_ref, rows_ref, stats_ref, held):
    _, cells, width, channels = tile_ref.shape
    side = weight_ref.shape[0]
    reach = side // 2
    lanes = 128
    total = jnp.zeros((cells, width, 1), jnp.float32)
    column = lax.broadcasted_iota(jnp.int32, (cells, width, lanes), 1)
    for group in range(channels // lanes):
        part = slice(group * lanes, (group + 1) * lanes)
        cell = tile_ref[0, :, :, part].astype(jnp.float32)
        sums = [
            jnp.broadcast_to(shift_ref[:, part], (width, lanes)) for _ in range(cells)
        ]
        for col_off in range(side):
            move = col_off - reach
            moved = cell
            if move:
                inside = (column + move >= 0) & (column + move < width)
                moved = jnp.where(inside, pltpu.roll(cell, (-move) % width, 1), 0.0)
            for row_off in range(side):
                scale = jnp.broadcast_to(
                    weight_ref[row_off, col_off : col_off + 1, part], (width, lanes)
                )
                for row in range(cells):
                    source = row + row_off - reach
                    if 0 <= source < cells:
                        sums[row] = sums[row] + moved[source] * scale
        out = jnp.stack(sums)
        held[:, :, part] = out
        total = total + jnp.sum(out, -1, keepdims=True)
    average = total / channels
    square = jnp.zeros((cells, width, 1), jnp.float32)
    for group in range(channels // lanes):
        part = slice(group * lanes, (group + 1) * lanes)
        centered = held[:, :, part] - average
        square = square + jnp.sum(centered * centered, -1, keepdims=True)
        rows_ref[0, :, :, part] = (centered * gain_ref[0, part]).astype(rows_ref.dtype)
    stats_ref[0, 0] = jnp.broadcast_to(average, (cells, width, lanes))
    stats_ref[1, 0] = jnp.broadcast_to(square, (cells, width, lanes))


def conv_rows(tiles, kernel, shift, gain):
    count, cells, width, channels = tiles.shape
    whole = pl.BlockSpec((1, channels), lambda t: (0, 0))
    return pl.pallas_call(
        conv_kernel,
        grid=(count,),
        in_specs=[
            pl.BlockSpec((1, cells, width, channels), lambda t: (t, 0, 0, 0)),
            pl.BlockSpec(kernel.shape, lambda t: (0, 0, 0)),
            whole,
            whole,
        ],
        out_specs=[
            pl.BlockSpec((1, cells, width, channels), lambda t: (t, 0, 0, 0)),
            pl.BlockSpec((2, 1, cells, width, 128), lambda t: (0, t, 0, 0, 0)),
        ],
        out_shape=[
            jax.ShapeDtypeStruct(tiles.shape, jnp.bfloat16),
            jax.ShapeDtypeStruct((2, count, cells, width, 128), jnp.float32),
        ],
        scratch_shapes=[pltpu.VMEM((cells, width, channels), jnp.float32)],
        compiler_params=pltpu.CompilerParams(vmem_limit_bytes=60 * 2**20),
    )(tiles, kernel, shift[None], gain[None])


def split_dot(rows, weight):
    parts = []
    rest = rows
    for _ in range(3):
        part = lax.reduce_precision(rest, 8, 7)
        parts.append(part)
        rest = rest - part
    stacked = jnp.concatenate(parts, 0).astype(jnp.bfloat16)
    out = jnp.dot(stacked, weight, preferred_element_type=jnp.float32)
    count = rows.shape[0]
    return out[:count] + out[count : 2 * count] + out[2 * count :]


def three_parts(value):
    first = value.astype(jnp.bfloat16).astype(jnp.float32)
    rest = value - first
    second = rest.astype(jnp.bfloat16).astype(jnp.float32)
    return first, second, rest - second


EXTRA = 16
STEP = 16


def project_kernel(rows_ref, weight_ref, out_ref):
    halves, _, columns = out_ref.shape
    width = columns // INNER
    for half in range(halves):
        for block in range(INNER):
            begin = (block * halves + half) * width
            out_ref[half, :, block * width : (block + 1) * width] = jnp.dot(
                rows_ref[...],
                weight_ref[:, begin : begin + width],
                preferred_element_type=jnp.float32,
            ).astype(out_ref.dtype)


def project(rows, weight, groups, halves):
    count, depth = rows.shape
    columns = weight.shape[1]
    return pl.pallas_call(
        project_kernel,
        grid=(groups,),
        in_specs=[
            pl.BlockSpec((count // groups, depth), lambda g: (g, 0)),
            pl.BlockSpec(weight.shape, lambda g: (0, 0)),
        ],
        out_specs=pl.BlockSpec((halves, count // groups, columns // halves), lambda g: (g, 0, 0)),
        out_shape=jax.ShapeDtypeStruct(
            (groups * halves, count // groups, columns // halves), jnp.bfloat16
        ),
        compiler_params=pltpu.CompilerParams(vmem_limit_bytes=60 * 2**20),
    )(rows, weight)


def kv_kernel(
    summed_ref, means_ref, squares_ref, gains_ref, bias_ref, unit_ref, scale_ref, weight_ref,
    out_ref, rows, stats,
):
    count, features = summed_ref.shape
    _, _, depth, lanes = weight_ref.shape
    n_seq = means_ref.shape[0]
    halves = out_ref.shape[0]
    own = count // halves
    width = out_ref.shape[3] // 2

    @pl.when(pl.program_id(0) == 0)
    def _():
        means = means_ref[...]
        average = jnp.sum(means, 0, keepdims=True) / n_seq
        offsets = means - average
        block = C // n_seq
        variance = (
            jnp.sum(squares_ref[...], 0, keepdims=True)
            + block * jnp.sum(offsets * offsets, 0, keepdims=True)
        ) / C
        inverse = lax.rsqrt(variance + epsilon)
        columns = jnp.transpose(
            jnp.concatenate([offsets, jnp.broadcast_to(inverse, (n_seq, count))], 0)
        )
        unit = unit_ref[...]
        gain = scale_ref[...]
        unit_square = jnp.sum(unit * unit)
        for begin in range(0, count, STEP):
            here = slice(begin, begin + STEP)
            value = summed_ref[here, :].astype(jnp.float32)
            for source in range(n_seq):
                value = value + columns[here, source : source + 1] * gains_ref[source : source + 1, :]
            value = value * columns[here, n_seq : n_seq + 1] + bias_ref[...]
            hidden = 0.5 * value * (1.0 + lax.erf(value * 0.7071067811865476))
            along = jnp.sum(hidden * unit, -1, keepdims=True)
            across = hidden - (along / unit_square) * unit
            square = jnp.sum(across * across, -1, keepdims=True)
            lane = lax.broadcasted_iota(jnp.int32, (STEP, 128), 1)
            stats[here, :] = jnp.where(lane == 0, along, jnp.where(lane == 1, square, unit_square))
            rows[here, :] = (across * gain).astype(jnp.bfloat16)
        rows[count:, :] = jnp.concatenate(
            [*three_parts(unit * gain), jnp.zeros((EXTRA - 3, features), jnp.float32)], 0
        ).astype(jnp.bfloat16)

    turned = jnp.transpose(stats[...])[:8]
    for pair in range(2):
        there = slice(pair * width, (pair + 1) * width)
        weight = jnp.concatenate(
            [
                weight_ref[(pair * 2 + side) * INNER : (pair * 2 + side + 1) * INNER, 0].reshape(
                    features, lanes
                )
                for side in range(width // lanes)
            ],
            1,
        )
        total = jnp.dot(rows[...], weight, preferred_element_type=jnp.float32)
        vector = total[count : count + 1] + total[count + 1 : count + 2] + total[count + 2 : count + 3]
        for half in range(halves):
            mine = slice(half * own, (half + 1) * own)
            out_ref[half, 0, :own, there] = total[mine].astype(out_ref.dtype)
            line = jnp.concatenate([turned[pair : pair + 1, mine], turned[2:3, mine]], 1)
            extra = jnp.concatenate(
                [
                    *three_parts(vector),
                    *three_parts(line),
                    jnp.zeros((EXTRA - 6, width), jnp.float32),
                ],
                0,
            )
            out_ref[half, 0, own:, there] = extra.astype(out_ref.dtype)


def kv_partial(summed, means, squares, gains, bias, unit, scale, weight, halves):
    count, features = summed.shape
    towers, groups, depth, lanes = weight.shape
    both = 4 * lanes
    rows_out = count // halves + EXTRA

    def whole(array):
        return pl.BlockSpec(array.shape, lambda g: (0,) * array.ndim)

    return pl.pallas_call(
        kv_kernel,
        grid=(groups,),
        in_specs=[
            *(whole(a) for a in (summed, means, squares, gains, bias, unit, scale)),
            pl.BlockSpec((towers, 1, depth, lanes), lambda g: (0, g, 0, 0)),
        ],
        out_specs=pl.BlockSpec((halves, 1, rows_out, both), lambda g: (0, g, 0, 0)),
        out_shape=jax.ShapeDtypeStruct((halves, groups, rows_out, both), jnp.bfloat16),
        scratch_shapes=[
            pltpu.VMEM((count + EXTRA, features), jnp.bfloat16),
            pltpu.VMEM((count, 128), jnp.float32),
        ],
        compiler_params=pltpu.CompilerParams(vmem_limit_bytes=60 * 2**20),
    )(summed, means, squares, gains, bias, unit, scale, weight)


def end_kernel(pieces_ref, bias_ref, cosine_ref, sine_ref, valid_ref, out_ref):
    groups, rows, both = pieces_ref.shape
    count = rows - EXTRA
    width = both // 2
    extra = pieces_ref[:, count:, :].astype(jnp.float32)
    vectors = extra[:, 0] + extra[:, 1] + extra[:, 2]
    lines = extra[:, 3] + extra[:, 4] + extra[:, 5]
    along = lines[:, :count]
    unit_square = lines[:, count : 2 * count]
    across = lines[:, width : width + count]
    coefficient = jnp.sum(along, 0, keepdims=True)
    left = along / unit_square - coefficient
    mean_square = jnp.sum(across + left * left * unit_square, 0, keepdims=True) / D
    inverse = lax.rsqrt(mean_square + epsilon)
    columns = jnp.transpose(
        jnp.concatenate([left, jnp.broadcast_to(inverse, (8, count))], 0)
    )
    total = jnp.zeros((count, both), jnp.float32)
    for group in range(groups):
        total = total + pieces_ref[group, :count].astype(jnp.float32)
        total = total + columns[:, group : group + 1] * vectors[group : group + 1, :]
    total = total * columns[:, groups : groups + 1]
    valid = valid_ref[...]
    for head in range(width // HEAD):
        there = slice(head * HEAD, (head + 1) * HEAD)
        key = total[:, there] + bias_ref[0:1, there]
        turned = key * cosine_ref[...] + pltpu.roll(key, HEAD // 2, 1) * sine_ref[...]
        out_ref[0, 0, :, there] = (turned * valid).astype(out_ref.dtype)
    value = total[:, width:] + bias_ref[1:2, :]
    out_ref[0, 1] = (value * valid[:, :1]).astype(out_ref.dtype)


def end_rows(pieces, bias, cosine, sine, valid):
    _, rows, both = pieces.shape
    return pl.pallas_call(
        end_kernel,
        out_shape=jax.ShapeDtypeStruct((1, 2, rows - EXTRA, both // 2), jnp.bfloat16),
        compiler_params=pltpu.CompilerParams(vmem_limit_bytes=60 * 2**20),
    )(pieces, bias, cosine, sine, valid)


def local(
    tiles,
    dw_weight,
    dw_bias,
    block_gain,
    block_bias,
    proj_weight,
    proj_bias,
    directions,
    dir_index,
    tile_counts,
    positions,
    rms_gain,
    kv_weight,
    kv_bias,
):
    n_row = lax.axis_size("row")
    n_half = lax.axis_size("half")
    n_mp = lax.axis_size("mp")
    n_seq = n_row * n_half
    half = lax.axis_index("half")

    block_rows, stats = conv_rows(tiles, dw_weight, dw_bias, block_gain)
    channels = tiles.shape[3]
    gathered = lax.all_gather(block_rows.reshape(-1, channels), "mp", axis=0, tiled=True)
    partial = project(gathered, proj_weight, n_row, n_half)
    partial, kv_weight = lax.optimization_barrier((partial, kv_weight))
    summed = lax.psum_scatter(partial, ("row", "half"), scatter_dimension=0, tiled=True)[0]

    pairs, depth, width = kv_weight.shape
    cut = lax.dynamic_slice_in_dim(kv_weight, half * (depth // n_half), depth // n_half, 1)
    sides = n_mp // pairs
    cut = cut.reshape(pairs, depth // n_half, sides, width // sides).swapaxes(1, 2)
    cut = cut.reshape(n_mp, depth // n_half, width // sides)
    cut = lax.all_to_all(
        cut,
        "tower",
        0,
        0,
        tiled=True,
        axis_index_groups=[[a * INNER + b for a in range(n_mp)] for b in range(INNER)],
    )
    cut = lax.all_to_all(cut, "mp", 0, 0, tiled=True)
    cut, stats, block_gain, block_bias = lax.optimization_barrier(
        (cut, stats, block_gain, block_bias)
    )
    kv_rows = lax.all_gather(cut, "tower", axis=0, tiled=False)

    vectors = split_dot(jnp.stack([block_gain, block_bias]), proj_weight)
    column_count = vectors.shape[1]
    own_count = column_count // n_half

    def own_half(row):
        row = row.reshape(INNER, n_half, -1)
        return lax.dynamic_index_in_dim(row, half, 1, False).reshape(-1)

    stats = stats[..., 0].reshape(2, -1)
    stats = lax.all_gather(stats, "mp", axis=1, tiled=True)
    rows_here = stats.shape[1] // n_row
    stats = stats.reshape(2, n_row, rows_here).swapaxes(0, 1).reshape(n_row, 1, -1)
    vectors = vectors.reshape(2, INNER, n_half, -1).transpose(2, 0, 1, 3).reshape(1, n_half, -1)
    payload = jnp.concatenate(
        [
            jnp.broadcast_to(stats, (n_row, n_half, stats.shape[2])),
            jnp.broadcast_to(vectors, (n_row, n_half, vectors.shape[2])),
        ],
        2,
    ).reshape(n_seq, -1)
    payload = lax.all_to_all(payload, ("row", "half"), 0, 0, tiled=True)
    means = payload[:, :rows_here]
    squares = payload[:, rows_here : 2 * rows_here]
    gain_rows = payload[:, 2 * rows_here : 2 * rows_here + own_count]
    bias_row = jnp.sum(payload[:, 2 * rows_here + own_count :], 0) + own_half(proj_bias)

    picked = jnp.arange(directions.shape[0], dtype=jnp.int32)[:, None] == dir_index[0]
    chosen = jnp.sum(jnp.where(picked, directions, 0.0), 0)
    unit_dir = chosen / jnp.sqrt(jnp.sum(chosen * chosen))
    local_unit = own_half(
        lax.dynamic_slice_in_dim(
            unit_dir, lax.axis_index("mp") * column_count, column_count, 0
        )
    )

    half_head = HEAD // 2
    inverse = jnp.power(
        jnp.float32(1000000.0), -(jnp.arange(half_head, dtype=jnp.float32) * 2.0 / HEAD)
    )
    angles = positions[0].astype(jnp.float32)[:, None] * inverse[None, :]
    cosine = jnp.tile(jnp.cos(angles), (1, 2))
    sine_part = jnp.sin(angles)
    sine = jnp.concatenate([-sine_part, sine_part], 1)
    out_rows = rows_here // n_half
    row_ids = (lax.axis_index("row") * n_half + half) * out_rows + jnp.arange(
        out_rows, dtype=jnp.int32
    )
    row_valid = (row_ids // (SIDE * SIDE) < tile_counts[0]).astype(jnp.float32)[:, None]
    row_valid = jnp.broadcast_to(row_valid, cosine.shape)

    pieces = kv_partial(
        summed,
        means,
        squares,
        gain_rows,
        bias_row[None],
        local_unit[None],
        own_half(rms_gain)[None],
        kv_rows,
        n_half,
    )
    pieces = pieces.reshape(n_half * n_mp, *pieces.shape[2:])
    pieces = lax.all_to_all(pieces, ("half", "mp"), 0, 0, tiled=True)
    return end_rows(pieces, kv_bias, cosine, sine, row_valid)


def solution(mesh):
    towers, seq, mp = mesh.devices.shape
    mesh = jax.sharding.Mesh(
        mesh.devices.reshape(towers, seq // 2, 2, mp), ("tower", "row", "half", "mp")
    )
    seq = ("row", "half")
    return jax.shard_map(
        local,
        mesh=mesh,
        in_specs=(
            P(("tower", "mp"), None, None, seq),
            P(None, None, seq),
            P(seq),
            P(seq),
            P(seq),
            P(seq, "mp"),
            P("mp"),
            P(),
            P("tower"),
            P("tower"),
            P("tower", seq),
            P("mp"),
            P(None, "tower", "mp"),
            P(None, "mp"),
        ),
        out_specs=P("tower", None, seq, "mp"),
        check_vma=False,
    )
```

```python
import jax
import jax.numpy as jnp
from jax import lax
from jax.experimental import pallas as pl
from jax.experimental.pallas import tpu as pltpu
from jax.sharding import PartitionSpec as P

C = 3072
D = 8192
HEAD = 128
SIDE = 8


epsilon = 1e-06


def conv_kernel(tile_ref, weight_ref, shift_ref, gain_ref, rows_ref, stats_ref, held):
    _, cells, width, channels = tile_ref.shape
    side = weight_ref.shape[0]
    reach = side // 2
    lanes = 128
    total = jnp.zeros((cells, width, 1), jnp.float32)
    column = lax.broadcasted_iota(jnp.int32, (cells, width, lanes), 1)
    for group in range(channels // lanes):
        part = slice(group * lanes, (group + 1) * lanes)
        cell = tile_ref[0, :, :, part].astype(jnp.float32)
        sums = [
            jnp.broadcast_to(shift_ref[:, part], (width, lanes)) for _ in range(cells)
        ]
        for col_off in range(side):
            move = col_off - reach
            moved = cell
            if move:
                inside = (column + move >= 0) & (column + move < width)
                moved = jnp.where(inside, pltpu.roll(cell, (-move) % width, 1), 0.0)
            for row_off in range(side):
                scale = jnp.broadcast_to(
                    weight_ref[row_off, col_off : col_off + 1, part], (width, lanes)
                )
                for row in range(cells):
                    source = row + row_off - reach
                    if 0 <= source < cells:
                        sums[row] = sums[row] + moved[source] * scale
        out = jnp.stack(sums)
        held[:, :, part] = out
        total = total + jnp.sum(out, -1, keepdims=True)
    average = total / channels
    square = jnp.zeros((cells, width, 1), jnp.float32)
    for group in range(channels // lanes):
        part = slice(group * lanes, (group + 1) * lanes)
        centered = held[:, :, part] - average
        square = square + jnp.sum(centered * centered, -1, keepdims=True)
        rows_ref[0, :, :, part] = (centered * gain_ref[0, part]).astype(rows_ref.dtype)
    stats_ref[0, 0] = jnp.broadcast_to(average, (cells, width, lanes))
    stats_ref[1, 0] = jnp.broadcast_to(square, (cells, width, lanes))


def conv_rows(tiles, kernel, shift, gain):
    count, cells, width, channels = tiles.shape
    whole = pl.BlockSpec((1, channels), lambda t: (0, 0))
    return pl.pallas_call(
        conv_kernel,
        grid=(count,),
        in_specs=[
            pl.BlockSpec((1, cells, width, channels), lambda t: (t, 0, 0, 0)),
            pl.BlockSpec(kernel.shape, lambda t: (0, 0, 0)),
            whole,
            whole,
        ],
        out_specs=[
            pl.BlockSpec((1, cells, width, channels), lambda t: (t, 0, 0, 0)),
            pl.BlockSpec((2, 1, cells, width, 128), lambda t: (0, t, 0, 0, 0)),
        ],
        out_shape=[
            jax.ShapeDtypeStruct(tiles.shape, jnp.bfloat16),
            jax.ShapeDtypeStruct((2, count, cells, width, 128), jnp.float32),
        ],
        scratch_shapes=[pltpu.VMEM((cells, width, channels), jnp.float32)],
        compiler_params=pltpu.CompilerParams(vmem_limit_bytes=32 * 2**20),
    )(tiles, kernel, shift[None], gain[None])


def split_dot(rows, weight):
    parts = []
    rest = rows
    for _ in range(3):
        part = lax.reduce_precision(rest, 8, 7)
        parts.append(part)
        rest = rest - part
    stacked = jnp.concatenate(parts, 0).astype(jnp.bfloat16)
    out = jnp.dot(stacked, weight, preferred_element_type=jnp.float32)
    count = rows.shape[0]
    return out[:count] + out[count : 2 * count] + out[2 * count :]


def three_parts(value):
    first = value.astype(jnp.bfloat16).astype(jnp.float32)
    rest = value - first
    second = rest.astype(jnp.bfloat16).astype(jnp.float32)
    return first, second, rest - second


EXTRA = 16
STEP = 16
PLACES = 8


def hidden_kernel(
    summed_ref, means_ref, squares_ref, gains_ref, bias_ref, unit_ref, scale_ref, rows_ref, sums_ref,
    stats,
):
    count, features = summed_ref.shape
    n_seq = means_ref.shape[0]
    depth = features // PLACES
    inner = PLACES // 2

    def store(here, value):
        for place in range(PLACES):
            source = (place % inner) * 2 + place // inner
            rows_ref[here, place * depth : (place + 1) * depth] = value[
                :, source * depth : (source + 1) * depth
            ]

    means = means_ref[...]
    average = jnp.sum(means, 0, keepdims=True) / n_seq
    offsets = means - average
    block = C // n_seq
    variance = (
        jnp.sum(squares_ref[...], 0, keepdims=True)
        + block * jnp.sum(offsets * offsets, 0, keepdims=True)
    ) / C
    inverse = lax.rsqrt(variance + epsilon)
    columns = jnp.transpose(
        jnp.concatenate([offsets, jnp.broadcast_to(inverse, (n_seq, count))], 0)
    )
    unit = unit_ref[...]
    gain = scale_ref[...]
    unit_square = jnp.sum(unit * unit)
    for begin in range(0, count, STEP):
        here = slice(begin, begin + STEP)
        value = summed_ref[here, :].astype(jnp.float32)
        for source in range(n_seq):
            value = value + columns[here, source : source + 1] * gains_ref[source : source + 1, :]
        value = value * columns[here, n_seq : n_seq + 1] + bias_ref[...]
        hidden = 0.5 * value * (1.0 + lax.erf(value * 0.7071067811865476))
        along = jnp.sum(hidden * unit, -1, keepdims=True)
        across = hidden - (along / unit_square) * unit
        square = jnp.sum(across * across, -1, keepdims=True)
        lane = lax.broadcasted_iota(jnp.int32, (STEP, count), 1)
        stats[here, :] = jnp.where(lane == 0, along, jnp.where(lane == 1, square, unit_square))
        store(here, (across * gain).astype(jnp.bfloat16))
    store(
        slice(count, count + EXTRA),
        jnp.concatenate(
            [*three_parts(unit * gain), jnp.zeros((EXTRA - 3, features), jnp.float32)], 0
        ).astype(jnp.bfloat16),
    )
    sums_ref[...] = jnp.transpose(stats[...])[:8]


def hidden_rows(summed, means, squares, gains, bias, unit, scale):
    count, features = summed.shape
    return pl.pallas_call(
        hidden_kernel,
        out_shape=[
            jax.ShapeDtypeStruct((count + EXTRA, features), jnp.bfloat16),
            jax.ShapeDtypeStruct((8, count), jnp.float32),
        ],
        scratch_shapes=[pltpu.VMEM((count, count), jnp.float32)],
        compiler_params=pltpu.CompilerParams(vmem_limit_bytes=32 * 2**20),
    )(summed, means, squares, gains, bias, unit, scale)


def kv_kernel(rows_ref, sums_ref, weight_ref, out_ref):
    count = rows_ref.shape[0] - EXTRA
    features = rows_ref.shape[1]
    width = weight_ref.shape[3]
    for pair in range(2):
        there = slice(pair * width, (pair + 1) * width)
        weight = weight_ref[pair * PLACES : (pair + 1) * PLACES, 0].reshape(features, width)
        total = jnp.dot(rows_ref[...], weight, preferred_element_type=jnp.float32)
        out_ref[0, :count, there] = total[:count].astype(out_ref.dtype)
        vector = total[count : count + 1] + total[count + 1 : count + 2] + total[count + 2 : count + 3]
        line = jnp.concatenate([sums_ref[pair : pair + 1], sums_ref[2:3]], 1)
        extra = jnp.concatenate(
            [
                *three_parts(vector),
                *three_parts(line),
                jnp.zeros((EXTRA - 6, width), jnp.float32),
            ],
            0,
        )
        out_ref[0, count:, there] = extra.astype(out_ref.dtype)


def kv_partial(rows, sums, weight):
    towers, groups, depth, width = weight.shape
    return pl.pallas_call(
        kv_kernel,
        grid=(groups,),
        in_specs=[
            pl.BlockSpec(rows.shape, lambda g: (0, 0)),
            pl.BlockSpec(sums.shape, lambda g: (0, 0)),
            pl.BlockSpec((towers, 1, depth, width), lambda g: (0, g, 0, 0)),
        ],
        out_specs=pl.BlockSpec((1, rows.shape[0], 2 * width), lambda g: (g, 0, 0)),
        out_shape=jax.ShapeDtypeStruct((groups, rows.shape[0], 2 * width), jnp.bfloat16),
        compiler_params=pltpu.CompilerParams(vmem_limit_bytes=58 * 2**20),
    )(rows, sums, weight)


def end_kernel(pieces_ref, bias_ref, cosine_ref, sine_ref, valid_ref, out_ref):
    groups, rows, both = pieces_ref.shape
    count = rows - EXTRA
    width = both // 2
    extra = pieces_ref[:, count:, :].astype(jnp.float32)
    vectors = extra[:, 0] + extra[:, 1] + extra[:, 2]
    lines = extra[:, 3] + extra[:, 4] + extra[:, 5]
    along = lines[:, :count]
    unit_square = lines[:, count : 2 * count]
    across = lines[:, width : width + count]
    coefficient = jnp.sum(along, 0, keepdims=True)
    left = along / unit_square - coefficient
    mean_square = jnp.sum(across + left * left * unit_square, 0, keepdims=True) / D
    inverse = lax.rsqrt(mean_square + epsilon)
    columns = jnp.transpose(
        jnp.concatenate([left, jnp.broadcast_to(inverse, (8 - groups, count))], 0)
    )
    total = jnp.zeros((count, both), jnp.float32)
    for group in range(groups):
        total = total + pieces_ref[group, :count].astype(jnp.float32)
        total = total + columns[:, group : group + 1] * vectors[group : group + 1, :]
    total = total * columns[:, groups : groups + 1]
    valid = valid_ref[...]
    for head in range(width // HEAD):
        there = slice(head * HEAD, (head + 1) * HEAD)
        key = total[:, there] + bias_ref[0:1, there]
        turned = key * cosine_ref[...] + pltpu.roll(key, HEAD // 2, 1) * sine_ref[...]
        out_ref[0, 0, :, there] = (turned * valid).astype(out_ref.dtype)
    value = total[:, width:] + bias_ref[1:2, :]
    out_ref[0, 1] = (value * valid[:, :1]).astype(out_ref.dtype)


def end_rows(pieces, bias, cosine, sine, valid):
    _, rows, both = pieces.shape
    return pl.pallas_call(
        end_kernel,
        out_shape=jax.ShapeDtypeStruct((1, 2, rows - EXTRA, both // 2), jnp.bfloat16),
        compiler_params=pltpu.CompilerParams(vmem_limit_bytes=32 * 2**20),
    )(pieces, bias, cosine, sine, valid)


def local(
    tiles,
    dw_weight,
    dw_bias,
    block_gain,
    block_bias,
    proj_weight,
    proj_bias,
    directions,
    dir_index,
    tile_counts,
    positions,
    rms_gain,
    kv_weight,
    kv_bias,
):
    n_seq = lax.axis_size("seq")
    n_mp = lax.axis_size("mp")
    n_tower = lax.axis_size("tower")
    pairs, depth, width = kv_weight.shape
    inner = n_tower // n_mp
    cut = kv_weight.reshape(n_mp, pairs * depth // n_mp, width)
    cut = lax.all_to_all(
        cut,
        "tower",
        0,
        0,
        tiled=True,
        axis_index_groups=[[a * inner + b for a in range(n_mp)] for b in range(inner)],
    )

    block_rows, stats = conv_rows(tiles, dw_weight, dw_bias, block_gain)
    channels = tiles.shape[3]
    gathered = lax.all_gather(block_rows.reshape(-1, channels), "mp", axis=0, tiled=True)
    gathered, cut = lax.optimization_barrier((gathered, cut))
    kv_rows = lax.all_gather(
        lax.all_to_all(cut, "mp", 0, 0, tiled=True), "tower", axis=0, tiled=False
    )
    partial = jnp.dot(gathered, proj_weight, preferred_element_type=jnp.float32).astype(
        jnp.bfloat16
    )
    partial, stats, block_gain, block_bias = lax.optimization_barrier(
        (partial, stats, block_gain, block_bias)
    )
    summed = lax.psum_scatter(partial, "seq", scatter_dimension=0, tiled=True)

    vectors = split_dot(jnp.stack([block_gain, block_bias]), proj_weight)
    stats = stats[..., 0].reshape(2, -1)
    stats = lax.all_gather(stats, "mp", axis=1, tiled=True)
    rows_here = stats.shape[1] // n_seq
    stats = stats.reshape(2, n_seq, rows_here).swapaxes(0, 1).reshape(n_seq, -1)
    payload = jnp.concatenate(
        [stats, jnp.broadcast_to(vectors.reshape(1, -1), (n_seq, vectors.size))], 1
    )
    payload = lax.all_to_all(payload, "seq", 0, 0, tiled=True)
    means = payload[:, :rows_here]
    squares = payload[:, rows_here : 2 * rows_here]
    column_count = vectors.shape[1]
    gain_rows = payload[:, 2 * rows_here : 2 * rows_here + column_count]
    bias_row = jnp.sum(payload[:, 2 * rows_here + column_count :], 0) + proj_bias

    picked = jnp.arange(directions.shape[0], dtype=jnp.int32)[:, None] == dir_index[0]
    chosen = jnp.sum(jnp.where(picked, directions, 0.0), 0)
    unit_dir = chosen / jnp.sqrt(jnp.sum(chosen * chosen))
    local_unit = lax.dynamic_slice_in_dim(
        unit_dir, lax.axis_index("mp") * column_count, column_count, 0
    )

    half_head = HEAD // 2
    inverse = jnp.power(
        jnp.float32(1000000.0), -(jnp.arange(half_head, dtype=jnp.float32) * 2.0 / HEAD)
    )
    angles = positions[0].astype(jnp.float32)[:, None] * inverse[None, :]
    cosine = jnp.tile(jnp.cos(angles), (1, 2))
    sine_part = jnp.sin(angles)
    sine = jnp.concatenate([-sine_part, sine_part], 1)
    row_ids = lax.axis_index("seq") * rows_here + jnp.arange(rows_here, dtype=jnp.int32)
    row_valid = (row_ids // (SIDE * SIDE) < tile_counts[0]).astype(jnp.float32)[:, None]
    row_valid = jnp.broadcast_to(row_valid, cosine.shape)

    rows, sums = hidden_rows(
        summed,
        means,
        squares,
        gain_rows,
        bias_row[None],
        local_unit[None],
        rms_gain[None],
    )
    pieces = kv_partial(rows, sums, kv_rows)
    pieces = lax.all_to_all(pieces, "mp", 0, 0, tiled=True)
    return end_rows(pieces, kv_bias, cosine, sine, row_valid)


def solution(mesh):
    return jax.shard_map(
        local,
        mesh=mesh,
        in_specs=(
            P(("tower", "mp"), None, None, "seq"),
            P(None, None, "seq"),
            P("seq"),
            P("seq"),
            P("seq"),
            P("seq", "mp"),
            P("mp"),
            P(),
            P("tower"),
            P("tower"),
            P("tower", "seq"),
            P("mp"),
            P(None, "tower", "mp"),
            P(None, "mp"),
        ),
        out_specs=P("tower", None, "seq", "mp"),
        check_vma=False,
    )
```

```python
import jax
import jax.numpy as jnp
from jax import lax
from jax.experimental import pallas as pl
from jax.experimental.pallas import tpu as pltpu
from jax.sharding import PartitionSpec as P

C = 3072
D = 8192
HEAD = 128
SIDE = 8
INNER = 4


epsilon = 1e-06


def conv_kernel(tile_ref, weight_ref, shift_ref, gain_ref, rows_ref, stats_ref, held):
    _, cells, width, channels = tile_ref.shape
    side = weight_ref.shape[0]
    reach = side // 2
    lanes = 128
    total = jnp.zeros((cells, width, 1), jnp.float32)
    column = lax.broadcasted_iota(jnp.int32, (cells, width, lanes), 1)
    for group in range(channels // lanes):
        part = slice(group * lanes, (group + 1) * lanes)
        cell = tile_ref[0, :, :, part].astype(jnp.float32)
        sums = [
            jnp.broadcast_to(shift_ref[part][None], (width, lanes)) for _ in range(cells)
        ]
        for col_off in range(side):
            move = col_off - reach
            moved = cell
            if move:
                inside = (column + move >= 0) & (column + move < width)
                moved = jnp.where(inside, pltpu.roll(cell, (-move) % width, 1), 0.0)
            for row_off in range(side):
                scale = jnp.broadcast_to(
                    weight_ref[row_off, col_off : col_off + 1, part], (width, lanes)
                )
                for row in range(cells):
                    source = row + row_off - reach
                    if 0 <= source < cells:
                        sums[row] = sums[row] + moved[source] * scale
        out = jnp.stack(sums)
        held[:, :, part] = out
        total = total + jnp.sum(out, -1, keepdims=True)
    average = total / channels
    square = jnp.zeros((cells, width, 1), jnp.float32)
    for group in range(channels // lanes):
        part = slice(group * lanes, (group + 1) * lanes)
        centered = held[:, :, part] - average
        square = square + jnp.sum(centered * centered, -1, keepdims=True)
        rows_ref[0, :, :, part] = (centered * gain_ref[part]).astype(rows_ref.dtype)
    stats_ref[0, 0] = jnp.broadcast_to(average, (cells, width, lanes))
    stats_ref[1, 0] = jnp.broadcast_to(square, (cells, width, lanes))


def conv_rows(tiles, kernel, shift, gain):
    count, cells, width, channels = tiles.shape
    whole = pl.BlockSpec((channels,), lambda t: (0,))
    return pl.pallas_call(
        conv_kernel,
        grid=(count,),
        in_specs=[
            pl.BlockSpec((1, cells, width, channels), lambda t: (t, 0, 0, 0)),
            pl.BlockSpec(kernel.shape, lambda t: (0, 0, 0)),
            whole,
            whole,
        ],
        out_specs=[
            pl.BlockSpec((1, cells, width, channels), lambda t: (t, 0, 0, 0)),
            pl.BlockSpec((2, 1, cells, width, 128), lambda t: (0, t, 0, 0, 0)),
        ],
        out_shape=[
            jax.ShapeDtypeStruct(tiles.shape, jnp.bfloat16),
            jax.ShapeDtypeStruct((2, count, cells, width, 128), jnp.float32),
        ],
        scratch_shapes=[pltpu.VMEM((cells, width, channels), jnp.float32)],
        compiler_params=pltpu.CompilerParams(vmem_limit_bytes=60 * 2**20),
    )(tiles, kernel, shift, gain)


def split_dot(rows, weight):
    parts = []
    rest = rows
    for _ in range(3):
        part = lax.reduce_precision(rest, 8, 7)
        parts.append(part)
        rest = rest - part
    stacked = jnp.concatenate(parts, 0).astype(jnp.bfloat16)
    out = jnp.dot(stacked, weight, preferred_element_type=jnp.float32)
    count = rows.shape[0]
    return out[:count] + out[count : 2 * count] + out[2 * count :]


def three_parts(value):
    first = value.astype(jnp.bfloat16).astype(jnp.float32)
    rest = value - first
    second = rest.astype(jnp.bfloat16).astype(jnp.float32)
    return first, second, rest - second


EXTRA = 16
STEP = 16


def project_kernel(rows_ref, weight_ref, out_ref):
    groups, _, count, _ = out_ref.shape
    for group in range(groups):
        out_ref[group, 0] = jnp.dot(
            rows_ref[group * count : (group + 1) * count, :],
            weight_ref[...],
            preferred_element_type=jnp.float32,
        ).astype(out_ref.dtype)


def project(rows, weight, groups, halves):
    count, depth = rows.shape
    columns = weight.shape[1]
    width = columns // (INNER * halves)
    out = pl.pallas_call(
        project_kernel,
        grid=(INNER * halves,),
        in_specs=[
            pl.BlockSpec((count, depth), lambda g: (0, 0)),
            pl.BlockSpec((depth, width), lambda g: (0, g)),
        ],
        out_specs=pl.BlockSpec(
            (groups, 1, count // groups, width), lambda g: (0, g % halves, 0, g // halves)
        ),
        out_shape=jax.ShapeDtypeStruct(
            (groups, halves, count // groups, columns // halves), jnp.bfloat16
        ),
        compiler_params=pltpu.CompilerParams(vmem_limit_bytes=60 * 2**20),
    )(rows, weight)
    return out.reshape(groups * halves, count // groups, columns // halves)


def hidden_kernel(
    summed_ref, means_ref, squares_ref, gains_ref, bias_ref, unit_ref, scale_ref, rows_ref, sums_ref,
    stats,
):
    count, features = summed_ref.shape
    n_seq = means_ref.shape[0]
    means = means_ref[...]
    average = jnp.sum(means, 0, keepdims=True) / n_seq
    offsets = means - average
    block = C // n_seq
    variance = (
        jnp.sum(squares_ref[...], 0, keepdims=True)
        + block * jnp.sum(offsets * offsets, 0, keepdims=True)
    ) / C
    inverse = lax.rsqrt(variance + epsilon)
    columns = jnp.transpose(
        jnp.concatenate([offsets, jnp.broadcast_to(inverse, (n_seq, count))], 0)
    )
    unit = unit_ref[...]
    gain = scale_ref[...]
    unit_square = jnp.sum(unit * unit)
    for begin in range(0, count, STEP):
        here = slice(begin, begin + STEP)
        value = summed_ref[here, :].astype(jnp.float32)
        for source in range(n_seq):
            value = value + columns[here, source : source + 1] * gains_ref[source : source + 1, :]
        value = value * columns[here, n_seq : n_seq + 1] + bias_ref[...]
        hidden = 0.5 * value * (1.0 + lax.erf(value * 0.7071067811865476))
        along = jnp.sum(hidden * unit, -1, keepdims=True)
        across = hidden - (along / unit_square) * unit
        square = jnp.sum(across * across, -1, keepdims=True)
        lane = lax.broadcasted_iota(jnp.int32, (STEP, 128), 1)
        stats[here, :] = jnp.where(lane == 0, along, jnp.where(lane == 1, square, unit_square))
        rows_ref[here, :] = (across * gain).astype(jnp.bfloat16)
    rows_ref[count:, :] = jnp.concatenate(
        [*three_parts(unit * gain), jnp.zeros((EXTRA - 3, features), jnp.float32)], 0
    ).astype(jnp.bfloat16)
    sums_ref[...] = jnp.transpose(stats[...])[:8]


def hidden_rows(summed, means, squares, gains, bias, unit, scale):
    count, features = summed.shape
    return pl.pallas_call(
        hidden_kernel,
        out_shape=[
            jax.ShapeDtypeStruct((count + EXTRA, features), jnp.bfloat16),
            jax.ShapeDtypeStruct((8, count), jnp.float32),
        ],
        scratch_shapes=[pltpu.VMEM((count, 128), jnp.float32)],
        compiler_params=pltpu.CompilerParams(vmem_limit_bytes=60 * 2**20),
    )(summed, means, squares, gains, bias, unit, scale)


def kv_kernel(rows_ref, sums_ref, weight_ref, out_ref):
    halves = out_ref.shape[0]
    features = rows_ref.shape[1]
    count = rows_ref.shape[0] - EXTRA
    own = count // halves
    width = weight_ref.shape[3]
    for pair in range(2):
        there = slice(pair * width, (pair + 1) * width)
        weight = weight_ref[:, pair].reshape(features, width)
        total = jnp.dot(rows_ref[...], weight, preferred_element_type=jnp.float32)
        vector = total[count : count + 1] + total[count + 1 : count + 2] + total[count + 2 : count + 3]
        for half in range(halves):
            mine = slice(half * own, (half + 1) * own)
            out_ref[half, 0, :own, there] = total[mine].astype(out_ref.dtype)
            line = jnp.concatenate([sums_ref[pair : pair + 1, mine], sums_ref[2:3, mine]], 1)
            extra = jnp.concatenate(
                [
                    *three_parts(vector),
                    *three_parts(line),
                    jnp.zeros((EXTRA - 6, width), jnp.float32),
                ],
                0,
            )
            out_ref[half, 0, own:, there] = extra.astype(out_ref.dtype)


def kv_partial(rows, sums, weight, halves):
    towers, pairs, depth, width = weight.shape
    groups = towers // INNER
    rows_out = (rows.shape[0] - EXTRA) // halves + EXTRA
    return pl.pallas_call(
        kv_kernel,
        grid=(groups,),
        in_specs=[
            pl.BlockSpec(rows.shape, lambda g: (0, 0)),
            pl.BlockSpec(sums.shape, lambda g: (0, 0)),
            pl.BlockSpec((INNER, pairs, depth, width), lambda g: (g, 0, 0, 0)),
        ],
        out_specs=pl.BlockSpec((halves, 1, rows_out, pairs * width), lambda g: (0, g, 0, 0)),
        out_shape=jax.ShapeDtypeStruct((halves, groups, rows_out, pairs * width), jnp.bfloat16),
        compiler_params=pltpu.CompilerParams(vmem_limit_bytes=60 * 2**20),
    )(rows, sums, weight)


def end_kernel(pieces_ref, bias_ref, cosine_ref, sine_ref, valid_ref, out_ref):
    groups, rows, both = pieces_ref.shape
    count = rows - EXTRA
    width = both // 2
    extra = pieces_ref[:, count:, :].astype(jnp.float32)
    vectors = extra[:, 0] + extra[:, 1] + extra[:, 2]
    lines = extra[:, 3] + extra[:, 4] + extra[:, 5]
    along = lines[:, :count]
    unit_square = lines[:, count : 2 * count]
    across = lines[:, width : width + count]
    coefficient = jnp.sum(along, 0, keepdims=True)
    left = along / unit_square - coefficient
    mean_square = jnp.sum(across + left * left * unit_square, 0, keepdims=True) / D
    inverse = lax.rsqrt(mean_square + epsilon)
    columns = jnp.transpose(
        jnp.concatenate([left, jnp.broadcast_to(inverse, (8, count))], 0)
    )
    total = jnp.zeros((count, both), jnp.float32)
    for group in range(groups):
        total = total + pieces_ref[group, :count].astype(jnp.float32)
        total = total + columns[:, group : group + 1] * vectors[group : group + 1, :]
    total = total * columns[:, groups : groups + 1]
    valid = valid_ref[...]
    for head in range(width // HEAD):
        there = slice(head * HEAD, (head + 1) * HEAD)
        key = total[:, there] + bias_ref[0:1, there]
        turned = key * cosine_ref[...] + pltpu.roll(key, HEAD // 2, 1) * sine_ref[...]
        out_ref[0, 0, :, there] = (turned * valid).astype(out_ref.dtype)
    value = total[:, width:] + bias_ref[1:2, :]
    out_ref[0, 1] = (value * valid[:, :1]).astype(out_ref.dtype)


def end_rows(pieces, bias, cosine, sine, valid):
    _, rows, both = pieces.shape
    return pl.pallas_call(
        end_kernel,
        out_shape=jax.ShapeDtypeStruct((1, 2, rows - EXTRA, both // 2), jnp.bfloat16),
        compiler_params=pltpu.CompilerParams(vmem_limit_bytes=32 * 2**20),
    )(pieces, bias, cosine, sine, valid)


def local(
    tiles,
    dw_weight,
    dw_bias,
    block_gain,
    block_bias,
    proj_weight,
    proj_bias,
    directions,
    dir_index,
    tile_counts,
    positions,
    rms_gain,
    kv_weight,
    kv_bias,
):
    n_row = lax.axis_size("row")
    n_half = lax.axis_size("half")
    n_mp = lax.axis_size("mp")
    n_seq = n_row * n_half
    half = lax.axis_index("half")

    block_rows, stats = conv_rows(tiles, dw_weight, dw_bias, block_gain)
    channels = tiles.shape[3]
    gathered = lax.all_gather(block_rows.reshape(-1, channels), "mp", axis=0, tiled=True)
    partial = project(gathered, proj_weight, n_row, n_half)
    partial, kv_weight = lax.optimization_barrier((partial, kv_weight))
    summed = lax.psum_scatter(partial, ("row", "half"), scatter_dimension=0, tiled=True)[0]

    depth = kv_weight.shape[1] // n_half
    swap = [
        ((a * INNER + b) * n_mp + x, (x * INNER + b) * n_mp + a)
        for a in range(n_mp)
        for b in range(INNER)
        for x in range(n_mp)
    ]
    cut = lax.dynamic_slice_in_dim(kv_weight, half * depth, depth, 1)
    cut = lax.ppermute(cut, ("tower", "mp"), swap)
    cut, stats, block_gain, block_bias = lax.optimization_barrier(
        (cut, stats, block_gain, block_bias)
    )
    kv_rows = lax.all_gather(cut, "tower", axis=0, tiled=False)

    vectors = split_dot(jnp.stack([block_gain, block_bias]), proj_weight)
    column_count = vectors.shape[1]
    own_count = column_count // n_half

    def own_half(row):
        row = row.reshape(INNER, n_half, -1)
        return lax.dynamic_index_in_dim(row, half, 1, False).reshape(-1)

    stats = stats[..., 0].reshape(2, -1)
    stats = lax.all_gather(stats, "mp", axis=1, tiled=True)
    rows_here = stats.shape[1] // n_row
    stats = stats.reshape(2, n_row, rows_here).swapaxes(0, 1).reshape(n_row, 1, -1)
    vectors = vectors.reshape(2, INNER, n_half, -1).transpose(2, 0, 1, 3).reshape(1, n_half, -1)
    payload = jnp.concatenate(
        [
            jnp.broadcast_to(stats, (n_row, n_half, stats.shape[2])),
            jnp.broadcast_to(vectors, (n_row, n_half, vectors.shape[2])),
        ],
        2,
    ).reshape(n_seq, -1)
    payload = lax.all_to_all(payload, ("row", "half"), 0, 0, tiled=True)
    means = payload[:, :rows_here]
    squares = payload[:, rows_here : 2 * rows_here]
    gain_rows = payload[:, 2 * rows_here : 2 * rows_here + own_count]
    bias_row = jnp.sum(payload[:, 2 * rows_here + own_count :], 0) + own_half(proj_bias)

    picked = jnp.arange(directions.shape[0], dtype=jnp.int32)[:, None] == dir_index[0]
    chosen = jnp.sum(jnp.where(picked, directions, 0.0), 0)
    unit_dir = chosen / jnp.sqrt(jnp.sum(chosen * chosen))
    local_unit = own_half(
        lax.dynamic_slice_in_dim(
            unit_dir, lax.axis_index("mp") * column_count, column_count, 0
        )
    )

    half_head = HEAD // 2
    inverse = jnp.power(
        jnp.float32(1000000.0), -(jnp.arange(half_head, dtype=jnp.float32) * 2.0 / HEAD)
    )
    angles = positions[0].astype(jnp.float32)[:, None] * inverse[None, :]
    cosine = jnp.tile(jnp.cos(angles), (1, 2))
    sine_part = jnp.sin(angles)
    sine = jnp.concatenate([-sine_part, sine_part], 1)
    out_rows = rows_here // n_half
    row_ids = (lax.axis_index("row") * n_half + half) * out_rows + jnp.arange(
        out_rows, dtype=jnp.int32
    )
    row_valid = (row_ids // (SIDE * SIDE) < tile_counts[0]).astype(jnp.float32)[:, None]
    row_valid = jnp.broadcast_to(row_valid, cosine.shape)

    rows, sums = hidden_rows(
        summed,
        means,
        squares,
        gain_rows,
        bias_row[None],
        local_unit[None],
        own_half(rms_gain)[None],
    )
    pieces = kv_partial(rows, sums, kv_rows, n_half)
    pieces = pieces.reshape(n_half * n_mp, *pieces.shape[2:])
    pieces = lax.all_to_all(pieces, ("half", "mp"), 0, 0, tiled=True)
    return end_rows(pieces, kv_bias, cosine, sine, row_valid)


def solution(mesh):
    towers, seq, mp = mesh.devices.shape
    mesh = jax.sharding.Mesh(
        mesh.devices.reshape(towers, seq // 2, 2, mp), ("tower", "row", "half", "mp")
    )
    seq = ("row", "half")
    return jax.shard_map(
        local,
        mesh=mesh,
        in_specs=(
            P(("tower", "mp"), None, None, seq),
            P(None, None, seq),
            P(seq),
            P(seq),
            P(seq),
            P(seq, "mp"),
            P("mp"),
            P(),
            P("tower"),
            P("tower"),
            P("tower", seq),
            P("mp"),
            P(None, "tower", "mp"),
            P(None, "mp"),
        ),
        out_specs=P("tower", None, seq, "mp"),
        check_vma=False,
    )
```

```python
import jax
import jax.numpy as jnp
from jax import lax
from jax.experimental import pallas as pl
from jax.experimental.pallas import tpu as pltpu
from jax.sharding import PartitionSpec as P

C = 3072
D = 8192
HEAD = 128
SIDE = 8
INNER = 4


epsilon = 1e-06


def conv_kernel(tile_ref, weight_ref, shift_ref, gain_ref, rows_ref, stats_ref, held):
    _, cells, width, channels = tile_ref.shape
    side = weight_ref.shape[0]
    reach = side // 2
    lanes = 128
    total = jnp.zeros((cells, width, 1), jnp.float32)
    column = lax.broadcasted_iota(jnp.int32, (cells, width, lanes), 1)
    for group in range(channels // lanes):
        part = slice(group * lanes, (group + 1) * lanes)
        cell = tile_ref[0, :, :, part].astype(jnp.float32)
        sums = [
            jnp.broadcast_to(shift_ref[part][None], (width, lanes)) for _ in range(cells)
        ]
        for col_off in range(side):
            move = col_off - reach
            moved = cell
            if move:
                inside = (column + move >= 0) & (column + move < width)
                moved = jnp.where(inside, pltpu.roll(cell, (-move) % width, 1), 0.0)
            for row_off in range(side):
                scale = jnp.broadcast_to(
                    weight_ref[row_off, col_off : col_off + 1, part], (width, lanes)
                )
                for row in range(cells):
                    source = row + row_off - reach
                    if 0 <= source < cells:
                        sums[row] = sums[row] + moved[source] * scale
        out = jnp.stack(sums)
        held[:, :, part] = out
        total = total + jnp.sum(out, -1, keepdims=True)
    average = total / channels
    square = jnp.zeros((cells, width, 1), jnp.float32)
    for group in range(channels // lanes):
        part = slice(group * lanes, (group + 1) * lanes)
        centered = held[:, :, part] - average
        square = square + jnp.sum(centered * centered, -1, keepdims=True)
        rows_ref[0, :, :, part] = (centered * gain_ref[part]).astype(rows_ref.dtype)
    stats_ref[0, 0] = jnp.broadcast_to(average, (cells, width, lanes))
    stats_ref[1, 0] = jnp.broadcast_to(square, (cells, width, lanes))


def conv_rows(tiles, kernel, shift, gain):
    count, cells, width, channels = tiles.shape
    whole = pl.BlockSpec((channels,), lambda t: (0,))
    return pl.pallas_call(
        conv_kernel,
        grid=(count,),
        in_specs=[
            pl.BlockSpec((1, cells, width, channels), lambda t: (t, 0, 0, 0)),
            pl.BlockSpec(kernel.shape, lambda t: (0, 0, 0)),
            whole,
            whole,
        ],
        out_specs=[
            pl.BlockSpec((1, cells, width, channels), lambda t: (t, 0, 0, 0)),
            pl.BlockSpec((2, 1, cells, width, 128), lambda t: (0, t, 0, 0, 0)),
        ],
        out_shape=[
            jax.ShapeDtypeStruct(tiles.shape, jnp.bfloat16),
            jax.ShapeDtypeStruct((2, count, cells, width, 128), jnp.float32),
        ],
        scratch_shapes=[pltpu.VMEM((cells, width, channels), jnp.float32)],
        compiler_params=pltpu.CompilerParams(vmem_limit_bytes=60 * 2**20),
    )(tiles, kernel, shift, gain)


def split_dot(rows, weight):
    parts = []
    rest = rows
    for _ in range(3):
        part = lax.reduce_precision(rest, 8, 7)
        parts.append(part)
        rest = rest - part
    stacked = jnp.concatenate(parts, 0).astype(jnp.bfloat16)
    out = jnp.dot(stacked, weight, preferred_element_type=jnp.float32)
    count = rows.shape[0]
    return out[:count] + out[count : 2 * count] + out[2 * count :]


def three_parts(value):
    first = value.astype(jnp.bfloat16).astype(jnp.float32)
    rest = value - first
    second = rest.astype(jnp.bfloat16).astype(jnp.float32)
    return first, second, rest - second


EXTRA = 16
STEP = 16


def project_kernel(rows_ref, weight_ref, out_ref):
    halves, _, columns = out_ref.shape
    width = columns // INNER
    for half in range(halves):
        for block in range(INNER):
            begin = (block * halves + half) * width
            out_ref[half, :, block * width : (block + 1) * width] = jnp.dot(
                rows_ref[...],
                weight_ref[:, begin : begin + width],
                preferred_element_type=jnp.float32,
            ).astype(out_ref.dtype)


def project(rows, weight, groups, halves):
    count, depth = rows.shape
    columns = weight.shape[1]
    return pl.pallas_call(
        project_kernel,
        grid=(groups,),
        in_specs=[
            pl.BlockSpec((count // groups, depth), lambda g: (g, 0)),
            pl.BlockSpec(weight.shape, lambda g: (0, 0)),
        ],
        out_specs=pl.BlockSpec((halves, count // groups, columns // halves), lambda g: (g, 0, 0)),
        out_shape=jax.ShapeDtypeStruct(
            (groups * halves, count // groups, columns // halves), jnp.bfloat16
        ),
        compiler_params=pltpu.CompilerParams(vmem_limit_bytes=60 * 2**20),
    )(rows, weight)


def hidden_kernel(
    summed_ref, means_ref, squares_ref, gains_ref, bias_ref, unit_ref, scale_ref, rows_ref, sums_ref,
    stats,
):
    count, features = summed_ref.shape
    n_seq = means_ref.shape[0]
    means = means_ref[...]
    average = jnp.sum(means, 0, keepdims=True) / n_seq
    offsets = means - average
    block = C // n_seq
    variance = (
        jnp.sum(squares_ref[...], 0, keepdims=True)
        + block * jnp.sum(offsets * offsets, 0, keepdims=True)
    ) / C
    inverse = lax.rsqrt(variance + epsilon)
    columns = jnp.transpose(
        jnp.concatenate([offsets, jnp.broadcast_to(inverse, (n_seq, count))], 0)
    )
    unit = unit_ref[...]
    gain = scale_ref[...]
    unit_square = jnp.sum(unit * unit)
    for begin in range(0, count, STEP):
        here = slice(begin, begin + STEP)
        value = summed_ref[here, :].astype(jnp.float32)
        for source in range(n_seq):
            value = value + columns[here, source : source + 1] * gains_ref[source : source + 1, :]
        value = value * columns[here, n_seq : n_seq + 1] + bias_ref[...]
        hidden = 0.5 * value * (1.0 + lax.erf(value * 0.7071067811865476))
        along = jnp.sum(hidden * unit, -1, keepdims=True)
        across = hidden - (along / unit_square) * unit
        square = jnp.sum(across * across, -1, keepdims=True)
        lane = lax.broadcasted_iota(jnp.int32, (STEP, 128), 1)
        stats[here, :] = jnp.where(lane == 0, along, jnp.where(lane == 1, square, unit_square))
        rows_ref[here, :] = (across * gain).astype(jnp.bfloat16)
    rows_ref[count:, :] = jnp.concatenate(
        [*three_parts(unit * gain), jnp.zeros((EXTRA - 3, features), jnp.float32)], 0
    ).astype(jnp.bfloat16)
    sums_ref[...] = jnp.transpose(stats[...])[:8]


def hidden_rows(summed, means, squares, gains, bias, unit, scale):
    count, features = summed.shape
    return pl.pallas_call(
        hidden_kernel,
        out_shape=[
            jax.ShapeDtypeStruct((count + EXTRA, features), jnp.bfloat16),
            jax.ShapeDtypeStruct((8, count), jnp.float32),
        ],
        scratch_shapes=[pltpu.VMEM((count, 128), jnp.float32)],
        compiler_params=pltpu.CompilerParams(vmem_limit_bytes=60 * 2**20),
    )(summed, means, squares, gains, bias, unit, scale)


def kv_kernel(rows_ref, sums_ref, weight_ref, out_ref):
    halves = out_ref.shape[0]
    features = rows_ref.shape[1]
    count = rows_ref.shape[0] - EXTRA
    own = count // halves
    width = weight_ref.shape[3]
    for pair in range(2):
        there = slice(pair * width, (pair + 1) * width)
        weight = weight_ref[:, pair].reshape(features, width)
        total = jnp.dot(rows_ref[...], weight, preferred_element_type=jnp.float32)
        vector = total[count : count + 1] + total[count + 1 : count + 2] + total[count + 2 : count + 3]
        for half in range(halves):
            mine = slice(half * own, (half + 1) * own)
            out_ref[half, 0, :own, there] = total[mine].astype(out_ref.dtype)
            line = jnp.concatenate([sums_ref[pair : pair + 1, mine], sums_ref[2:3, mine]], 1)
            extra = jnp.concatenate(
                [
                    *three_parts(vector),
                    *three_parts(line),
                    jnp.zeros((EXTRA - 6, width), jnp.float32),
                ],
                0,
            )
            out_ref[half, 0, own:, there] = extra.astype(out_ref.dtype)


def kv_partial(rows, sums, weight, halves):
    towers, pairs, depth, width = weight.shape
    groups = towers // INNER
    rows_out = (rows.shape[0] - EXTRA) // halves + EXTRA
    return pl.pallas_call(
        kv_kernel,
        grid=(groups,),
        in_specs=[
            pl.BlockSpec(rows.shape, lambda g: (0, 0)),
            pl.BlockSpec(sums.shape, lambda g: (0, 0)),
            pl.BlockSpec((INNER, pairs, depth, width), lambda g: (g, 0, 0, 0)),
        ],
        out_specs=pl.BlockSpec((halves, 1, rows_out, pairs * width), lambda g: (0, g, 0, 0)),
        out_shape=jax.ShapeDtypeStruct((halves, groups, rows_out, pairs * width), jnp.bfloat16),
        compiler_params=pltpu.CompilerParams(vmem_limit_bytes=60 * 2**20),
    )(rows, sums, weight)


def end_kernel(pieces_ref, bias_ref, cosine_ref, sine_ref, valid_ref, out_ref):
    groups, rows, both = pieces_ref.shape
    count = rows - EXTRA
    width = both // 2
    extra = pieces_ref[:, count:, :].astype(jnp.float32)
    vectors = extra[:, 0] + extra[:, 1] + extra[:, 2]
    lines = extra[:, 3] + extra[:, 4] + extra[:, 5]
    along = lines[:, :count]
    unit_square = lines[:, count : 2 * count]
    across = lines[:, width : width + count]
    coefficient = jnp.sum(along, 0, keepdims=True)
    left = along / unit_square - coefficient
    mean_square = jnp.sum(across + left * left * unit_square, 0, keepdims=True) / D
    inverse = lax.rsqrt(mean_square + epsilon)
    columns = jnp.transpose(
        jnp.concatenate([left, jnp.broadcast_to(inverse, (8, count))], 0)
    )
    total = jnp.zeros((count, both), jnp.float32)
    for group in range(groups):
        total = total + pieces_ref[group, :count].astype(jnp.float32)
        total = total + columns[:, group : group + 1] * vectors[group : group + 1, :]
    total = total * columns[:, groups : groups + 1]
    valid = valid_ref[...]
    for head in range(width // HEAD):
        there = slice(head * HEAD, (head + 1) * HEAD)
        key = total[:, there] + bias_ref[0:1, there]
        turned = key * cosine_ref[...] + pltpu.roll(key, HEAD // 2, 1) * sine_ref[...]
        out_ref[0, 0, :, there] = (turned * valid).astype(out_ref.dtype)
    value = total[:, width:] + bias_ref[1:2, :]
    out_ref[0, 1] = (value * valid[:, :1]).astype(out_ref.dtype)


def end_rows(pieces, bias, cosine, sine, valid):
    _, rows, both = pieces.shape
    return pl.pallas_call(
        end_kernel,
        out_shape=jax.ShapeDtypeStruct((1, 2, rows - EXTRA, both // 2), jnp.bfloat16),
        compiler_params=pltpu.CompilerParams(vmem_limit_bytes=32 * 2**20),
    )(pieces, bias, cosine, sine, valid)


def local(
    tiles,
    dw_weight,
    dw_bias,
    block_gain,
    block_bias,
    proj_weight,
    proj_bias,
    directions,
    dir_index,
    tile_counts,
    positions,
    rms_gain,
    kv_weight,
    kv_bias,
):
    n_row = lax.axis_size("row")
    n_half = lax.axis_size("half")
    n_mp = lax.axis_size("mp")
    n_seq = n_row * n_half
    half = lax.axis_index("half")

    block_rows, stats = conv_rows(tiles, dw_weight, dw_bias, block_gain)
    channels = tiles.shape[3]
    gathered = lax.all_gather(block_rows.reshape(-1, channels), "mp", axis=0, tiled=True)
    partial = project(gathered, proj_weight, n_row, n_half)
    partial, kv_weight = lax.optimization_barrier((partial, kv_weight))
    summed = lax.psum_scatter(partial, ("row", "half"), scatter_dimension=0, tiled=True)[0]

    depth = kv_weight.shape[1] // n_half
    swap = [
        ((a * INNER + b) * n_mp + x, (x * INNER + b) * n_mp + a)
        for a in range(n_mp)
        for b in range(INNER)
        for x in range(n_mp)
    ]
    cut = lax.dynamic_slice_in_dim(kv_weight, half * depth, depth, 1)
    cut = lax.ppermute(cut, ("tower", "mp"), swap)
    cut, stats, block_gain, block_bias = lax.optimization_barrier(
        (cut, stats, block_gain, block_bias)
    )
    kv_rows = lax.all_gather(cut, "tower", axis=0, tiled=False)

    vectors = split_dot(jnp.stack([block_gain, block_bias]), proj_weight)
    column_count = vectors.shape[1]
    own_count = column_count // n_half

    def own_half(row):
        row = row.reshape(INNER, n_half, -1)
        return lax.dynamic_index_in_dim(row, half, 1, False).reshape(-1)

    stats = stats[..., 0].reshape(2, -1)
    stats = lax.all_gather(stats, "mp", axis=1, tiled=True)
    rows_here = stats.shape[1] // n_row
    stats = stats.reshape(2, n_row, rows_here).swapaxes(0, 1).reshape(n_row, 1, -1)
    vectors = vectors.reshape(2, INNER, n_half, -1).transpose(2, 0, 1, 3).reshape(1, n_half, -1)
    payload = jnp.concatenate(
        [
            jnp.broadcast_to(stats, (n_row, n_half, stats.shape[2])),
            jnp.broadcast_to(vectors, (n_row, n_half, vectors.shape[2])),
        ],
        2,
    ).reshape(n_seq, -1)
    payload = lax.all_to_all(payload, ("row", "half"), 0, 0, tiled=True)
    means = payload[:, :rows_here]
    squares = payload[:, rows_here : 2 * rows_here]
    gain_rows = payload[:, 2 * rows_here : 2 * rows_here + own_count]
    bias_row = jnp.sum(payload[:, 2 * rows_here + own_count :], 0) + own_half(proj_bias)

    picked = jnp.arange(directions.shape[0], dtype=jnp.int32)[:, None] == dir_index[0]
    chosen = jnp.sum(jnp.where(picked, directions, 0.0), 0)
    unit_dir = chosen / jnp.sqrt(jnp.sum(chosen * chosen))
    local_unit = own_half(
        lax.dynamic_slice_in_dim(
            unit_dir, lax.axis_index("mp") * column_count, column_count, 0
        )
    )

    half_head = HEAD // 2
    inverse = jnp.power(
        jnp.float32(1000000.0), -(jnp.arange(half_head, dtype=jnp.float32) * 2.0 / HEAD)
    )
    angles = positions[0].astype(jnp.float32)[:, None] * inverse[None, :]
    cosine = jnp.tile(jnp.cos(angles), (1, 2))
    sine_part = jnp.sin(angles)
    sine = jnp.concatenate([-sine_part, sine_part], 1)
    out_rows = rows_here // n_half
    row_ids = (lax.axis_index("row") * n_half + half) * out_rows + jnp.arange(
        out_rows, dtype=jnp.int32
    )
    row_valid = (row_ids // (SIDE * SIDE) < tile_counts[0]).astype(jnp.float32)[:, None]
    row_valid = jnp.broadcast_to(row_valid, cosine.shape)

    rows, sums = hidden_rows(
        summed,
        means,
        squares,
        gain_rows,
        bias_row[None],
        local_unit[None],
        own_half(rms_gain)[None],
    )
    pieces = kv_partial(rows, sums, kv_rows, n_half)
    pieces = pieces.reshape(n_half * n_mp, *pieces.shape[2:])
    pieces = lax.all_to_all(pieces, ("half", "mp"), 0, 0, tiled=True)
    return end_rows(pieces, kv_bias, cosine, sine, row_valid)


def solution(mesh):
    towers, seq, mp = mesh.devices.shape
    mesh = jax.sharding.Mesh(
        mesh.devices.reshape(towers, seq // 2, 2, mp), ("tower", "row", "half", "mp")
    )
    seq = ("row", "half")
    return jax.shard_map(
        local,
        mesh=mesh,
        in_specs=(
            P(("tower", "mp"), None, None, seq),
            P(None, None, seq),
            P(seq),
            P(seq),
            P(seq),
            P(seq, "mp"),
            P("mp"),
            P(),
            P("tower"),
            P("tower"),
            P("tower", seq),
            P("mp"),
            P(None, "tower", "mp"),
            P(None, "mp"),
        ),
        out_specs=P("tower", None, seq, "mp"),
        check_vma=False,
    )
```

```python
import functools

import jax
import jax.numpy as jnp
from jax import lax
from jax.experimental import pallas as pl
from jax.experimental.pallas import tpu as pltpu
from jax.sharding import PartitionSpec as P

C = 3072
D = 8192
HEAD = 128
SIDE = 8
INNER = 4


epsilon = 1e-06


def conv_kernel(tile_ref, weight_ref, shift_ref, gain_ref, rows_ref, stats_ref, held):
    _, cells, width, channels = tile_ref.shape
    side = weight_ref.shape[0]
    reach = side // 2
    lanes = 128
    total = jnp.zeros((cells, width, 1), jnp.float32)
    column = lax.broadcasted_iota(jnp.int32, (cells, width, lanes), 1)
    for group in range(channels // lanes):
        part = slice(group * lanes, (group + 1) * lanes)
        cell = tile_ref[0, :, :, part].astype(jnp.float32)
        sums = [
            jnp.broadcast_to(shift_ref[part][None], (width, lanes)) for _ in range(cells)
        ]
        for col_off in range(side):
            move = col_off - reach
            moved = cell
            if move:
                inside = (column + move >= 0) & (column + move < width)
                moved = jnp.where(inside, pltpu.roll(cell, (-move) % width, 1), 0.0)
            for row_off in range(side):
                scale = jnp.broadcast_to(
                    weight_ref[row_off, col_off : col_off + 1, part], (width, lanes)
                )
                for row in range(cells):
                    source = row + row_off - reach
                    if 0 <= source < cells:
                        sums[row] = sums[row] + moved[source] * scale
        out = jnp.stack(sums)
        held[:, :, part] = out
        total = total + jnp.sum(out, -1, keepdims=True)
    average = total / channels
    square = jnp.zeros((cells, width, 1), jnp.float32)
    for group in range(channels // lanes):
        part = slice(group * lanes, (group + 1) * lanes)
        centered = held[:, :, part] - average
        square = square + jnp.sum(centered * centered, -1, keepdims=True)
        rows_ref[0, :, :, part] = (centered * gain_ref[part]).astype(rows_ref.dtype)
    stats_ref[0, 0] = jnp.broadcast_to(average, (cells, width, lanes))
    stats_ref[1, 0] = jnp.broadcast_to(square, (cells, width, lanes))


def conv_rows(tiles, kernel, shift, gain):
    count, cells, width, channels = tiles.shape
    whole = pl.BlockSpec((channels,), lambda t: (0,))
    return pl.pallas_call(
        conv_kernel,
        grid=(count,),
        in_specs=[
            pl.BlockSpec((1, cells, width, channels), lambda t: (t, 0, 0, 0)),
            pl.BlockSpec(kernel.shape, lambda t: (0, 0, 0)),
            whole,
            whole,
        ],
        out_specs=[
            pl.BlockSpec((1, cells, width, channels), lambda t: (t, 0, 0, 0)),
            pl.BlockSpec((2, 1, cells, width, 128), lambda t: (0, t, 0, 0, 0)),
        ],
        out_shape=[
            jax.ShapeDtypeStruct(tiles.shape, jnp.bfloat16),
            jax.ShapeDtypeStruct((2, count, cells, width, 128), jnp.float32),
        ],
        scratch_shapes=[pltpu.VMEM((cells, width, channels), jnp.float32)],
        compiler_params=pltpu.CompilerParams(vmem_limit_bytes=60 * 2**20),
    )(tiles, kernel, shift, gain)


def split_dot(rows, weight):
    parts = []
    rest = rows
    for _ in range(3):
        part = lax.reduce_precision(rest, 8, 7)
        parts.append(part)
        rest = rest - part
    stacked = jnp.concatenate(parts, 0).astype(jnp.bfloat16)
    out = jnp.dot(stacked, weight, preferred_element_type=jnp.float32)
    count = rows.shape[0]
    return out[:count] + out[count : 2 * count] + out[2 * count :]


def three_parts(value):
    first = value.astype(jnp.bfloat16).astype(jnp.float32)
    rest = value - first
    second = rest.astype(jnp.bfloat16).astype(jnp.float32)
    return first, second, rest - second


EXTRA = 16
STEP = 16


def project_kernel(rows_ref, weight_ref, out_ref):
    halves, _, columns = out_ref.shape
    width = columns // INNER
    for half in range(halves):
        for block in range(INNER):
            begin = (block * halves + half) * width
            out_ref[half, :, block * width : (block + 1) * width] = jnp.dot(
                rows_ref[...],
                weight_ref[:, begin : begin + width],
                preferred_element_type=jnp.float32,
            ).astype(out_ref.dtype)


def project(rows, weight, groups, halves):
    count, depth = rows.shape
    columns = weight.shape[1]
    return pl.pallas_call(
        project_kernel,
        grid=(groups,),
        in_specs=[
            pl.BlockSpec((count // groups, depth), lambda g: (g, 0)),
            pl.BlockSpec(weight.shape, lambda g: (0, 0)),
        ],
        out_specs=pl.BlockSpec((halves, count // groups, columns // halves), lambda g: (g, 0, 0)),
        out_shape=jax.ShapeDtypeStruct(
            (groups * halves, count // groups, columns // halves), jnp.bfloat16
        ),
        compiler_params=pltpu.CompilerParams(vmem_limit_bytes=60 * 2**20),
    )(rows, weight)


def hidden_kernel(
    summed_ref, means_ref, squares_ref, gains_ref, bias_ref, unit_ref, scale_ref, rows_ref, sums_ref,
    stats,
):
    count, features = summed_ref.shape
    n_seq = means_ref.shape[0]
    means = means_ref[...]
    average = jnp.sum(means, 0, keepdims=True) / n_seq
    offsets = means - average
    block = C // n_seq
    variance = (
        jnp.sum(squares_ref[...], 0, keepdims=True)
        + block * jnp.sum(offsets * offsets, 0, keepdims=True)
    ) / C
    inverse = lax.rsqrt(variance + epsilon)
    columns = jnp.transpose(
        jnp.concatenate([offsets, jnp.broadcast_to(inverse, (n_seq, count))], 0)
    )
    unit = unit_ref[...]
    gain = scale_ref[...]
    unit_square = jnp.sum(unit * unit)
    for begin in range(0, count, STEP):
        here = slice(begin, begin + STEP)
        value = summed_ref[here, :].astype(jnp.float32)
        for source in range(n_seq):
            value = value + columns[here, source : source + 1] * gains_ref[source : source + 1, :]
        value = value * columns[here, n_seq : n_seq + 1] + bias_ref[...]
        hidden = 0.5 * value * (1.0 + lax.erf(value * 0.7071067811865476))
        along = jnp.sum(hidden * unit, -1, keepdims=True)
        across = hidden - (along / unit_square) * unit
        square = jnp.sum(across * across, -1, keepdims=True)
        lane = lax.broadcasted_iota(jnp.int32, (STEP, 128), 1)
        stats[here, :] = jnp.where(lane == 0, along, jnp.where(lane == 1, square, unit_square))
        rows_ref[here, :] = (across * gain).astype(jnp.bfloat16)
    rows_ref[count:, :] = jnp.concatenate(
        [*three_parts(unit * gain), jnp.zeros((EXTRA - 3, features), jnp.float32)], 0
    ).astype(jnp.bfloat16)
    sums_ref[...] = jnp.transpose(stats[...])[:8]


def hidden_rows(summed, means, squares, gains, bias, unit, scale):
    count, features = summed.shape
    return pl.pallas_call(
        hidden_kernel,
        out_shape=[
            jax.ShapeDtypeStruct((count + EXTRA, features), jnp.bfloat16),
            jax.ShapeDtypeStruct((8, count), jnp.float32),
        ],
        scratch_shapes=[pltpu.VMEM((count, 128), jnp.float32)],
        compiler_params=pltpu.CompilerParams(vmem_limit_bytes=60 * 2**20),
    )(summed, means, squares, gains, bias, unit, scale)


def kv_kernel(pair, rows_ref, sums_ref, weight_ref, *refs):
    out_ref = refs[-1]
    halves = out_ref.shape[0]
    features = rows_ref.shape[1]
    count = rows_ref.shape[0] - EXTRA
    own = count // halves
    width = weight_ref.shape[2]
    weight = weight_ref[...].reshape(features, width)
    total = jnp.dot(rows_ref[...], weight, preferred_element_type=jnp.float32)
    vector = total[count : count + 1] + total[count + 1 : count + 2] + total[count + 2 : count + 3]
    for half in range(halves):
        mine = slice(half * own, (half + 1) * own)
        out_ref[half, 0, :own, :] = total[mine].astype(out_ref.dtype)
        line = jnp.concatenate([sums_ref[pair : pair + 1, mine], sums_ref[2:3, mine]], 1)
        extra = jnp.concatenate(
            [
                *three_parts(vector),
                *three_parts(line),
                jnp.zeros((EXTRA - 6, width), jnp.float32),
            ],
            0,
        )
        out_ref[half, 0, own:, :] = extra.astype(out_ref.dtype)


def kv_partial(rows, sums, weight, halves, pair, held=None):
    towers, depth, width = weight.shape
    groups = towers // INNER
    rows_out = (rows.shape[0] - EXTRA) // halves + EXTRA
    in_specs = [
        pl.BlockSpec(rows.shape, lambda g: (0, 0)),
        pl.BlockSpec(sums.shape, lambda g: (0, 0)),
        pl.BlockSpec((INNER, depth, width), lambda g: (g, 0, 0)),
    ]
    operands = [rows, sums, weight]
    aliases = {}
    if held is not None:
        in_specs.append(pl.BlockSpec(memory_space=pl.ANY))
        operands.append(held)
        aliases = {3: 0}
    return pl.pallas_call(
        functools.partial(kv_kernel, pair),
        grid=(groups,),
        in_specs=in_specs,
        out_specs=pl.BlockSpec((halves, 1, rows_out, width), lambda g: (0, g, 0, pair)),
        out_shape=jax.ShapeDtypeStruct((halves, groups, rows_out, 2 * width), jnp.bfloat16),
        input_output_aliases=aliases,
        compiler_params=pltpu.CompilerParams(vmem_limit_bytes=60 * 2**20),
    )(*operands)


def end_kernel(pieces_ref, bias_ref, cosine_ref, sine_ref, valid_ref, out_ref):
    groups, rows, both = pieces_ref.shape
    count = rows - EXTRA
    width = both // 2
    extra = pieces_ref[:, count:, :].astype(jnp.float32)
    vectors = extra[:, 0] + extra[:, 1] + extra[:, 2]
    lines = extra[:, 3] + extra[:, 4] + extra[:, 5]
    along = lines[:, :count]
    unit_square = lines[:, count : 2 * count]
    across = lines[:, width : width + count]
    coefficient = jnp.sum(along, 0, keepdims=True)
    left = along / unit_square - coefficient
    mean_square = jnp.sum(across + left * left * unit_square, 0, keepdims=True) / D
    inverse = lax.rsqrt(mean_square + epsilon)
    columns = jnp.transpose(
        jnp.concatenate([left, jnp.broadcast_to(inverse, (8, count))], 0)
    )
    total = jnp.zeros((count, both), jnp.float32)
    for group in range(groups):
        total = total + pieces_ref[group, :count].astype(jnp.float32)
        total = total + columns[:, group : group + 1] * vectors[group : group + 1, :]
    total = total * columns[:, groups : groups + 1]
    valid = valid_ref[...]
    for head in range(width // HEAD):
        there = slice(head * HEAD, (head + 1) * HEAD)
        key = total[:, there] + bias_ref[0:1, there]
        turned = key * cosine_ref[...] + pltpu.roll(key, HEAD // 2, 1) * sine_ref[...]
        out_ref[0, 0, :, there] = (turned * valid).astype(out_ref.dtype)
    value = total[:, width:] + bias_ref[1:2, :]
    out_ref[0, 1] = (value * valid[:, :1]).astype(out_ref.dtype)


def end_rows(pieces, bias, cosine, sine, valid):
    _, rows, both = pieces.shape
    return pl.pallas_call(
        end_kernel,
        out_shape=jax.ShapeDtypeStruct((1, 2, rows - EXTRA, both // 2), jnp.bfloat16),
        compiler_params=pltpu.CompilerParams(vmem_limit_bytes=32 * 2**20),
    )(pieces, bias, cosine, sine, valid)


def local(
    tiles,
    dw_weight,
    dw_bias,
    block_gain,
    block_bias,
    proj_weight,
    proj_bias,
    directions,
    dir_index,
    tile_counts,
    positions,
    rms_gain,
    kv_weight,
    kv_bias,
):
    n_row = lax.axis_size("row")
    n_half = lax.axis_size("half")
    n_mp = lax.axis_size("mp")
    n_seq = n_row * n_half
    half = lax.axis_index("half")

    block_rows, stats = conv_rows(tiles, dw_weight, dw_bias, block_gain)
    channels = tiles.shape[3]
    gathered = lax.all_gather(block_rows.reshape(-1, channels), "mp", axis=0, tiled=True)
    partial = project(gathered, proj_weight, n_row, n_half)
    partial, kv_weight = lax.optimization_barrier((partial, kv_weight))
    summed = lax.psum_scatter(partial, ("row", "half"), scatter_dimension=0, tiled=True)[0]

    depth = kv_weight.shape[1] // n_half
    swap = [
        ((a * INNER + b) * n_mp + x, (x * INNER + b) * n_mp + a)
        for a in range(n_mp)
        for b in range(INNER)
        for x in range(n_mp)
    ]
    cut = lax.dynamic_slice_in_dim(kv_weight, half * depth, depth, 1)
    key_cut, value_cut = lax.optimization_barrier((cut[0], cut[1]))
    key_cut = lax.ppermute(key_cut, ("tower", "mp"), swap)
    key_cut, value_cut = lax.optimization_barrier((key_cut, value_cut))
    key_weight = lax.all_gather(key_cut, "tower", axis=0, tiled=False)
    value_cut = lax.ppermute(value_cut, ("tower", "mp"), swap)
    value_cut, stats, block_gain, block_bias = lax.optimization_barrier(
        (value_cut, stats, block_gain, block_bias)
    )
    value_weight = lax.all_gather(value_cut, "tower", axis=0, tiled=False)

    vectors = split_dot(jnp.stack([block_gain, block_bias]), proj_weight)
    column_count = vectors.shape[1]
    own_count = column_count // n_half

    def own_half(row):
        row = row.reshape(INNER, n_half, -1)
        return lax.dynamic_index_in_dim(row, half, 1, False).reshape(-1)

    stats = stats[..., 0].reshape(2, -1)
    stats = lax.all_gather(stats, "mp", axis=1, tiled=True)
    rows_here = stats.shape[1] // n_row
    stats = stats.reshape(2, n_row, rows_here).swapaxes(0, 1).reshape(n_row, 1, -1)
    vectors = vectors.reshape(2, INNER, n_half, -1).transpose(2, 0, 1, 3).reshape(1, n_half, -1)
    payload = jnp.concatenate(
        [
            jnp.broadcast_to(stats, (n_row, n_half, stats.shape[2])),
            jnp.broadcast_to(vectors, (n_row, n_half, vectors.shape[2])),
        ],
        2,
    ).reshape(n_seq, -1)
    payload = lax.all_to_all(payload, ("row", "half"), 0, 0, tiled=True)
    means = payload[:, :rows_here]
    squares = payload[:, rows_here : 2 * rows_here]
    gain_rows = payload[:, 2 * rows_here : 2 * rows_here + own_count]
    bias_row = jnp.sum(payload[:, 2 * rows_here + own_count :], 0) + own_half(proj_bias)

    picked = jnp.arange(directions.shape[0], dtype=jnp.int32)[:, None] == dir_index[0]
    chosen = jnp.sum(jnp.where(picked, directions, 0.0), 0)
    unit_dir = chosen / jnp.sqrt(jnp.sum(chosen * chosen))
    local_unit = own_half(
        lax.dynamic_slice_in_dim(
            unit_dir, lax.axis_index("mp") * column_count, column_count, 0
        )
    )

    half_head = HEAD // 2
    inverse = jnp.power(
        jnp.float32(1000000.0), -(jnp.arange(half_head, dtype=jnp.float32) * 2.0 / HEAD)
    )
    angles = positions[0].astype(jnp.float32)[:, None] * inverse[None, :]
    cosine = jnp.tile(jnp.cos(angles), (1, 2))
    sine_part = jnp.sin(angles)
    sine = jnp.concatenate([-sine_part, sine_part], 1)
    out_rows = rows_here // n_half
    row_ids = (lax.axis_index("row") * n_half + half) * out_rows + jnp.arange(
        out_rows, dtype=jnp.int32
    )
    row_valid = (row_ids // (SIDE * SIDE) < tile_counts[0]).astype(jnp.float32)[:, None]
    row_valid = jnp.broadcast_to(row_valid, cosine.shape)

    rows, sums = hidden_rows(
        summed,
        means,
        squares,
        gain_rows,
        bias_row[None],
        local_unit[None],
        own_half(rms_gain)[None],
    )
    pieces = kv_partial(rows, sums, key_weight, n_half, 0)
    pieces = kv_partial(rows, sums, value_weight, n_half, 1, pieces)
    pieces = pieces.reshape(n_half * n_mp, *pieces.shape[2:])
    pieces = lax.all_to_all(pieces, ("half", "mp"), 0, 0, tiled=True)
    return end_rows(pieces, kv_bias, cosine, sine, row_valid)


def solution(mesh):
    towers, seq, mp = mesh.devices.shape
    mesh = jax.sharding.Mesh(
        mesh.devices.reshape(towers, seq // 2, 2, mp), ("tower", "row", "half", "mp")
    )
    seq = ("row", "half")
    return jax.shard_map(
        local,
        mesh=mesh,
        in_specs=(
            P(("tower", "mp"), None, None, seq),
            P(None, None, seq),
            P(seq),
            P(seq),
            P(seq),
            P(seq, "mp"),
            P("mp"),
            P(),
            P("tower"),
            P("tower"),
            P("tower", seq),
            P("mp"),
            P(None, "tower", "mp"),
            P(None, "mp"),
        ),
        out_specs=P("tower", None, seq, "mp"),
        check_vma=False,
    )
```

```python
import jax
import jax.numpy as jnp
from jax import lax
from jax.experimental import pallas as pl
from jax.experimental.pallas import tpu as pltpu
from jax.sharding import PartitionSpec as P

C = 3072
D = 8192
HEAD = 128
SIDE = 8
INNER = 4


epsilon = 1e-06


TILES = 4


def conv_kernel(tile_ref, weight_ref, shift_ref, gain_ref, rows_ref, stats_ref, held):
    count, cells, width, channels = tile_ref.shape
    side = weight_ref.shape[0]
    reach = side // 2
    lanes = 128
    column = lax.broadcasted_iota(jnp.int32, (cells, width, lanes), 1)
    for tile in range(count):
        total = jnp.zeros((cells, width, 1), jnp.float32)
        for group in range(channels // lanes):
            part = slice(group * lanes, (group + 1) * lanes)
            cell = tile_ref[tile, :, :, part].astype(jnp.float32)
            sums = [
                jnp.broadcast_to(shift_ref[part][None], (width, lanes)) for _ in range(cells)
            ]
            for col_off in range(side):
                move = col_off - reach
                moved = cell
                if move:
                    inside = (column + move >= 0) & (column + move < width)
                    moved = jnp.where(inside, pltpu.roll(cell, (-move) % width, 1), 0.0)
                for row_off in range(side):
                    scale = jnp.broadcast_to(
                        weight_ref[row_off, col_off : col_off + 1, part], (width, lanes)
                    )
                    for row in range(cells):
                        source = row + row_off - reach
                        if 0 <= source < cells:
                            sums[row] = sums[row] + moved[source] * scale
            out = jnp.stack(sums)
            held[:, :, part] = out
            total = total + jnp.sum(out, -1, keepdims=True)
        average = total / channels
        square = jnp.zeros((cells, width, 1), jnp.float32)
        for group in range(channels // lanes):
            part = slice(group * lanes, (group + 1) * lanes)
            centered = held[:, :, part] - average
            square = square + jnp.sum(centered * centered, -1, keepdims=True)
            rows_ref[tile, :, :, part] = (centered * gain_ref[part]).astype(rows_ref.dtype)
        stats_ref[0, tile] = jnp.broadcast_to(average, (cells, width, lanes))
        stats_ref[1, tile] = jnp.broadcast_to(square, (cells, width, lanes))


def conv_rows(tiles, kernel, shift, gain):
    count, cells, width, channels = tiles.shape
    whole = pl.BlockSpec((channels,), lambda t: (0,))
    return pl.pallas_call(
        conv_kernel,
        grid=(count // TILES,),
        in_specs=[
            pl.BlockSpec((TILES, cells, width, channels), lambda t: (t, 0, 0, 0)),
            pl.BlockSpec(kernel.shape, lambda t: (0, 0, 0)),
            whole,
            whole,
        ],
        out_specs=[
            pl.BlockSpec((TILES, cells, width, channels), lambda t: (t, 0, 0, 0)),
            pl.BlockSpec((2, TILES, cells, width, 128), lambda t: (0, t, 0, 0, 0)),
        ],
        out_shape=[
            jax.ShapeDtypeStruct(tiles.shape, jnp.bfloat16),
            jax.ShapeDtypeStruct((2, count, cells, width, 128), jnp.float32),
        ],
        scratch_shapes=[pltpu.VMEM((cells, width, channels), jnp.float32)],
        compiler_params=pltpu.CompilerParams(vmem_limit_bytes=60 * 2**20),
    )(tiles, kernel, shift, gain)


def split_dot(rows, weight):
    parts = []
    rest = rows
    for _ in range(3):
        part = lax.reduce_precision(rest, 8, 7)
        parts.append(part)
        rest = rest - part
    stacked = jnp.concatenate(parts, 0).astype(jnp.bfloat16)
    out = jnp.dot(stacked, weight, preferred_element_type=jnp.float32)
    count = rows.shape[0]
    return out[:count] + out[count : 2 * count] + out[2 * count :]


def three_parts(value):
    first = value.astype(jnp.bfloat16).astype(jnp.float32)
    rest = value - first
    second = rest.astype(jnp.bfloat16).astype(jnp.float32)
    return first, second, rest - second


EXTRA = 16
STEP = 16


def project_kernel(rows_ref, weight_ref, out_ref):
    chunks, count, columns = out_ref.shape
    parts = rows_ref.shape[0] // count
    halves = chunks // parts
    width = columns // INNER
    for part in range(parts):
        for half in range(halves):
            for block in range(INNER):
                begin = (block * halves + half) * width
                out_ref[part * halves + half, :, block * width : (block + 1) * width] = jnp.dot(
                    rows_ref[part * count : (part + 1) * count, :],
                    weight_ref[:, begin : begin + width],
                    preferred_element_type=jnp.float32,
                ).astype(out_ref.dtype)


def project(rows, weight, groups, halves):
    count, depth = rows.shape
    columns = weight.shape[1]
    parts = 2
    chunks = parts * halves
    return pl.pallas_call(
        project_kernel,
        grid=(groups // parts,),
        in_specs=[
            pl.BlockSpec((count // groups * parts, depth), lambda g: (g, 0)),
            pl.BlockSpec(weight.shape, lambda g: (0, 0)),
        ],
        out_specs=pl.BlockSpec((chunks, count // groups, columns // halves), lambda g: (g, 0, 0)),
        out_shape=jax.ShapeDtypeStruct(
            (groups * halves, count // groups, columns // halves), jnp.bfloat16
        ),
        compiler_params=pltpu.CompilerParams(vmem_limit_bytes=60 * 2**20),
    )(rows, weight)


def hidden_kernel(
    summed_ref, means_ref, squares_ref, gains_ref, bias_ref, unit_ref, scale_ref, rows_ref, sums_ref,
    stats,
):
    count, features = summed_ref.shape
    n_seq = means_ref.shape[0]
    means = means_ref[...]
    average = jnp.sum(means, 0, keepdims=True) / n_seq
    offsets = means - average
    block = C // n_seq
    variance = (
        jnp.sum(squares_ref[...], 0, keepdims=True)
        + block * jnp.sum(offsets * offsets, 0, keepdims=True)
    ) / C
    inverse = lax.rsqrt(variance + epsilon)
    columns = jnp.transpose(
        jnp.concatenate([offsets, jnp.broadcast_to(inverse, (n_seq, count))], 0)
    )
    unit = unit_ref[...]
    gain = scale_ref[...]
    unit_square = jnp.sum(unit * unit)
    for begin in range(0, count, STEP):
        here = slice(begin, begin + STEP)
        value = summed_ref[here, :].astype(jnp.float32)
        for source in range(n_seq):
            value = value + columns[here, source : source + 1] * gains_ref[source : source + 1, :]
        value = value * columns[here, n_seq : n_seq + 1] + bias_ref[...]
        hidden = 0.5 * value * (1.0 + lax.erf(value * 0.7071067811865476))
        along = jnp.sum(hidden * unit, -1, keepdims=True)
        across = hidden - (along / unit_square) * unit
        square = jnp.sum(across * across, -1, keepdims=True)
        lane = lax.broadcasted_iota(jnp.int32, (STEP, 128), 1)
        stats[here, :] = jnp.where(lane == 0, along, jnp.where(lane == 1, square, unit_square))
        rows_ref[here, :] = (across * gain).astype(jnp.bfloat16)
    rows_ref[count:, :] = jnp.concatenate(
        [*three_parts(unit * gain), jnp.zeros((EXTRA - 3, features), jnp.float32)], 0
    ).astype(jnp.bfloat16)
    sums_ref[...] = jnp.transpose(stats[...])[:8]


def hidden_rows(summed, means, squares, gains, bias, unit, scale):
    count, features = summed.shape
    return pl.pallas_call(
        hidden_kernel,
        out_shape=[
            jax.ShapeDtypeStruct((count + EXTRA, features), jnp.bfloat16),
            jax.ShapeDtypeStruct((8, count), jnp.float32),
        ],
        scratch_shapes=[pltpu.VMEM((count, 128), jnp.float32)],
        compiler_params=pltpu.CompilerParams(vmem_limit_bytes=60 * 2**20),
    )(summed, means, squares, gains, bias, unit, scale)


def kv_kernel(rows_ref, sums_ref, weight_ref, out_ref):
    halves = out_ref.shape[0]
    features = rows_ref.shape[1]
    count = rows_ref.shape[0] - EXTRA
    own = count // halves
    width = weight_ref.shape[3]
    for pair in range(2):
        there = slice(pair * width, (pair + 1) * width)
        weight = weight_ref[:, pair].reshape(features, width)
        total = jnp.dot(rows_ref[...], weight, preferred_element_type=jnp.float32)
        vector = total[count : count + 1] + total[count + 1 : count + 2] + total[count + 2 : count + 3]
        for half in range(halves):
            mine = slice(half * own, (half + 1) * own)
            out_ref[half, 0, :own, there] = total[mine].astype(out_ref.dtype)
            line = jnp.concatenate([sums_ref[pair : pair + 1, mine], sums_ref[2:3, mine]], 1)
            extra = jnp.concatenate(
                [
                    *three_parts(vector),
                    *three_parts(line),
                    jnp.zeros((EXTRA - 6, width), jnp.float32),
                ],
                0,
            )
            out_ref[half, 0, own:, there] = extra.astype(out_ref.dtype)


def kv_partial(rows, sums, weight, halves):
    towers, pairs, depth, width = weight.shape
    groups = towers // INNER
    rows_out = (rows.shape[0] - EXTRA) // halves + EXTRA
    return pl.pallas_call(
        kv_kernel,
        grid=(groups,),
        in_specs=[
            pl.BlockSpec(rows.shape, lambda g: (0, 0)),
            pl.BlockSpec(sums.shape, lambda g: (0, 0)),
            pl.BlockSpec((INNER, pairs, depth, width), lambda g: (g, 0, 0, 0)),
        ],
        out_specs=pl.BlockSpec((halves, 1, rows_out, pairs * width), lambda g: (0, g, 0, 0)),
        out_shape=jax.ShapeDtypeStruct((halves, groups, rows_out, pairs * width), jnp.bfloat16),
        compiler_params=pltpu.CompilerParams(vmem_limit_bytes=60 * 2**20),
    )(rows, sums, weight)


def end_kernel(pieces_ref, bias_ref, cosine_ref, sine_ref, valid_ref, out_ref):
    groups, rows, both = pieces_ref.shape
    count = rows - EXTRA
    width = both // 2
    extra = pieces_ref[:, count:, :].astype(jnp.float32)
    vectors = extra[:, 0] + extra[:, 1] + extra[:, 2]
    lines = extra[:, 3] + extra[:, 4] + extra[:, 5]
    along = lines[:, :count]
    unit_square = lines[:, count : 2 * count]
    across = lines[:, width : width + count]
    coefficient = jnp.sum(along, 0, keepdims=True)
    left = along / unit_square - coefficient
    mean_square = jnp.sum(across + left * left * unit_square, 0, keepdims=True) / D
    inverse = lax.rsqrt(mean_square + epsilon)
    columns = jnp.transpose(
        jnp.concatenate([left, jnp.broadcast_to(inverse, (8, count))], 0)
    )
    total = jnp.zeros((count, both), jnp.float32)
    for group in range(groups):
        total = total + pieces_ref[group, :count].astype(jnp.float32)
        total = total + columns[:, group : group + 1] * vectors[group : group + 1, :]
    total = total * columns[:, groups : groups + 1]
    valid = valid_ref[...]
    for head in range(width // HEAD):
        there = slice(head * HEAD, (head + 1) * HEAD)
        key = total[:, there] + bias_ref[0:1, there]
        turned = key * cosine_ref[...] + pltpu.roll(key, HEAD // 2, 1) * sine_ref[...]
        out_ref[0, 0, :, there] = (turned * valid).astype(out_ref.dtype)
    value = total[:, width:] + bias_ref[1:2, :]
    out_ref[0, 1] = (value * valid[:, :1]).astype(out_ref.dtype)


def end_rows(pieces, bias, cosine, sine, valid):
    _, rows, both = pieces.shape
    return pl.pallas_call(
        end_kernel,
        out_shape=jax.ShapeDtypeStruct((1, 2, rows - EXTRA, both // 2), jnp.bfloat16),
        compiler_params=pltpu.CompilerParams(vmem_limit_bytes=32 * 2**20),
    )(pieces, bias, cosine, sine, valid)


def local(
    tiles,
    dw_weight,
    dw_bias,
    block_gain,
    block_bias,
    proj_weight,
    proj_bias,
    directions,
    dir_index,
    tile_counts,
    positions,
    rms_gain,
    kv_weight,
    kv_bias,
):
    n_row = lax.axis_size("row")
    n_half = lax.axis_size("half")
    n_mp = lax.axis_size("mp")
    n_seq = n_row * n_half
    half = lax.axis_index("half")

    block_rows, stats = conv_rows(tiles, dw_weight, dw_bias, block_gain)
    channels = tiles.shape[3]
    gathered = lax.all_gather(block_rows.reshape(-1, channels), "mp", axis=0, tiled=True)
    partial = project(gathered, proj_weight, n_row, n_half)
    partial, kv_weight = lax.optimization_barrier((partial, kv_weight))
    summed = lax.psum_scatter(partial, ("row", "half"), scatter_dimension=0, tiled=True)[0]

    depth = kv_weight.shape[1] // n_half
    swap = [
        ((a * INNER + b) * n_mp + x, (x * INNER + b) * n_mp + a)
        for a in range(n_mp)
        for b in range(INNER)
        for x in range(n_mp)
    ]
    cut = lax.dynamic_slice_in_dim(kv_weight, half * depth, depth, 1)
    cut = lax.ppermute(cut, ("tower", "mp"), swap)
    cut, stats, block_gain, block_bias = lax.optimization_barrier(
        (cut, stats, block_gain, block_bias)
    )
    kv_rows = lax.all_gather(cut, "tower", axis=0, tiled=False)

    vectors = split_dot(jnp.stack([block_gain, block_bias]), proj_weight)
    column_count = vectors.shape[1]
    own_count = column_count // n_half

    def own_half(row):
        row = row.reshape(INNER, n_half, -1)
        return lax.dynamic_index_in_dim(row, half, 1, False).reshape(-1)

    stats = stats[..., 0].reshape(2, -1)
    stats = lax.all_gather(stats, "mp", axis=1, tiled=True)
    rows_here = stats.shape[1] // n_row
    stats = stats.reshape(2, n_row, rows_here).swapaxes(0, 1).reshape(n_row, 1, -1)
    vectors = vectors.reshape(2, INNER, n_half, -1).transpose(2, 0, 1, 3).reshape(1, n_half, -1)
    payload = jnp.concatenate(
        [
            jnp.broadcast_to(stats, (n_row, n_half, stats.shape[2])),
            jnp.broadcast_to(vectors, (n_row, n_half, vectors.shape[2])),
        ],
        2,
    ).reshape(n_seq, -1)
    payload = lax.all_to_all(payload, ("row", "half"), 0, 0, tiled=True)
    means = payload[:, :rows_here]
    squares = payload[:, rows_here : 2 * rows_here]
    gain_rows = payload[:, 2 * rows_here : 2 * rows_here + own_count]
    bias_row = jnp.sum(payload[:, 2 * rows_here + own_count :], 0) + own_half(proj_bias)

    picked = jnp.arange(directions.shape[0], dtype=jnp.int32)[:, None] == dir_index[0]
    chosen = jnp.sum(jnp.where(picked, directions, 0.0), 0)
    unit_dir = chosen / jnp.sqrt(jnp.sum(chosen * chosen))
    local_unit = own_half(
        lax.dynamic_slice_in_dim(
            unit_dir, lax.axis_index("mp") * column_count, column_count, 0
        )
    )

    half_head = HEAD // 2
    inverse = jnp.power(
        jnp.float32(1000000.0), -(jnp.arange(half_head, dtype=jnp.float32) * 2.0 / HEAD)
    )
    angles = positions[0].astype(jnp.float32)[:, None] * inverse[None, :]
    cosine = jnp.tile(jnp.cos(angles), (1, 2))
    sine_part = jnp.sin(angles)
    sine = jnp.concatenate([-sine_part, sine_part], 1)
    out_rows = rows_here // n_half
    row_ids = (lax.axis_index("row") * n_half + half) * out_rows + jnp.arange(
        out_rows, dtype=jnp.int32
    )
    row_valid = (row_ids // (SIDE * SIDE) < tile_counts[0]).astype(jnp.float32)[:, None]
    row_valid = jnp.broadcast_to(row_valid, cosine.shape)

    rows, sums = hidden_rows(
        summed,
        means,
        squares,
        gain_rows,
        bias_row[None],
        local_unit[None],
        own_half(rms_gain)[None],
    )
    pieces = kv_partial(rows, sums, kv_rows, n_half)
    pieces = pieces.reshape(n_half * n_mp, *pieces.shape[2:])
    pieces = lax.all_to_all(pieces, ("half", "mp"), 0, 0, tiled=True)
    return end_rows(pieces, kv_bias, cosine, sine, row_valid)


def solution(mesh):
    towers, seq, mp = mesh.devices.shape
    mesh = jax.sharding.Mesh(
        mesh.devices.reshape(towers, seq // 2, 2, mp), ("tower", "row", "half", "mp")
    )
    seq = ("row", "half")
    return jax.shard_map(
        local,
        mesh=mesh,
        in_specs=(
            P(("tower", "mp"), None, None, seq),
            P(None, None, seq),
            P(seq),
            P(seq),
            P(seq),
            P(seq, "mp"),
            P("mp"),
            P(),
            P("tower"),
            P("tower"),
            P("tower", seq),
            P("mp"),
            P(None, "tower", "mp"),
            P(None, "mp"),
        ),
        out_specs=P("tower", None, seq, "mp"),
        check_vma=False,
    )
```
